32 devices in a mesh: pop: 4 (over z), tp: 8 (over y, x, core).
Axes of the slice: x: 2, y: 2, z: 4, core: 2. Of those that a mesh axis runs over, the one named last changes fastest.
Arguments:
- in_spikes: int32 [4, 15, 4096], replicated, may hold values 0 or 1
- w_in: bfloat16 [4096, 4096], P(None, 'tp'), may hold values from -0.1875 to 0.1875
- w_rec: bfloat16 [4096, 4096], P(None, 'tp'), may hold values from -0.1875 to 0.1875
- leak_rate: float32 [4096], P('tp'), may hold values from 0.5 to 0.95
- neuron_bias: float32 [4096], P('tp'), may hold values from -2.5 to 2.5
- readout: float32 [4096], P('tp'), may hold values from -0.1875 to 0.1875
- pert_table: bfloat16 [256, 4096], P(None, 'tp'), may hold values from -4 to 4
- pert_idx: int32 [128, 2], P('pop'), may hold values from 0 to 255
- member_ranks: int32 [128], P('pop'), may hold values from 0 to 127, each once
Outputs:
- returns: float32 [128], P('pop')
- grad_rec: bfloat16 [4096, 4096], P(None, 'tp')
The draws below stay inside these ranges and needn't reach their ends.
Inputs may be any that keep to these rules, and one draw needn't show every extreme that they name: member_ranks holds each of 0 to 127 once.
All inputs are finite; a program needn't handle non-finite values.
Results may differ from the reference program's by a relative error of at most 0.0044.
Values may be sent and summed in bfloat16 or wider, within the bound.
No kernel may reach another device: no remote copies, remote signals or barrier semaphores. Data moves between devices by JAX's collectives and lax.ppermute only.
A program may use at most 64 MiB of HBM per device.

```python
import jax
import jax.numpy as jnp
from jax import lax

NEUR = 4096
INP = 4096
KTAB = 256
STEPS = 4
EPIS = 15
MEMBERS = 128


def plant(array, stream_key, least, high):
    longest = array.shape.index(max(array.shape))
    spots = []
    for shift in (0, 1):
        where = [jax.random.randint(jax.random.fold_in(stream_key, axis), (), 0, length) for axis, length in enumerate(array.shape)]
        where[longest] = (where[longest] + shift) % array.shape[longest]
        spots.append(tuple(where))
    return array.at[spots[0]].set(least).at[spots[1]].set(high)


def shard_levels(key, dims, shards, smallest, largest):
    factor_of = 1.0
    for axis_at, blocks in shards:
        draws = jax.random.uniform(jax.random.fold_in(jax.random.fold_in(key, 6), axis_at), (blocks,), jnp.float32, smallest / len(shards), largest / len(shards))
        factor_of = factor_of * jnp.repeat(jnp.exp(draws), dims[axis_at] // blocks).reshape((-1,) + (1,) * (len(dims) - 1 - axis_at))
    return factor_of


def scatter_about(key, extent, spread, limit, cuts=(), dtype=jnp.bfloat16):
    array = jax.random.normal(key, extent, jnp.float32) * spread
    if len(cuts) > 0:
        array = shard_levels(key, extent, cuts, -0.22, 0.18) * array
    return jnp.clip(array, min=-limit, max=limit).astype(dtype)


def setup_inputs(seed: int = 0) -> dict:
    arg_keys = jax.random.split(jax.random.key(seed), 10)
    in_spikes = plant((jax.random.randint(arg_keys[0], (STEPS, EPIS, INP), 0, 4) < 1).astype(jnp.int32), jax.random.fold_in(arg_keys[0], 1), 0, 1)
    w_in = scatter_about(arg_keys[1], (INP, NEUR), (INP // 4) ** -0.5, 0.1875, ((1, 8),))
    w_rec = scatter_about(arg_keys[2], (NEUR, NEUR), (NEUR // 4) ** -0.5, 0.1875, ((1, 8),))
    leak_rate = jnp.clip(0.5 + 0.45 * jax.random.uniform(arg_keys[3], (NEUR,), jnp.float32) ** shard_levels(arg_keys[3], (NEUR,), ((0, 8),), -0.2, 0.2), 0.5, 0.95)
    neuron_bias = scatter_about(arg_keys[4], (NEUR,), 0.5, 2.5, ((0, 8),), jnp.float32)
    readout = scatter_about(arg_keys[5], (NEUR,), (NEUR // 4) ** -0.5, 0.1875, ((0, 8),), jnp.float32)
    pert_table = scatter_about(arg_keys[6], (KTAB, NEUR), 1.0, 4.0, ((1, 8),))
    pert_idx = plant(jax.random.randint(arg_keys[7], (MEMBERS, 2), 0, KTAB), jax.random.fold_in(arg_keys[7], 1), 0, KTAB - 1).astype(jnp.int32)
    member_ranks = jax.random.permutation(arg_keys[8], MEMBERS).astype(jnp.int32)
    return {"in_spikes": in_spikes, "w_in": w_in, "w_rec": w_rec, "leak_rate": leak_rate, "neuron_bias": neuron_bias, "readout": readout, "pert_table": pert_table, "pert_idx": pert_idx, "member_ranks": member_ranks}


sigma_scale = 0.01

def reference(in_spikes, w_in, w_rec, leak_rate, neuron_bias, readout, pert_table, pert_idx, member_ranks):
    member_count = pert_idx.shape[0]
    spike_input = in_spikes.astype(jnp.bfloat16).reshape(STEPS * EPIS, INP)
    input_drive = jnp.dot(spike_input, w_in, preferred_element_type=jnp.float32) + neuron_bias
    input_drive = input_drive.reshape(STEPS, EPIS, NEUR)
    pre_side = jnp.take(pert_table, pert_idx[:, 0], axis=0)
    post_side = jnp.take(pert_table, pert_idx[:, 1], axis=0).astype(jnp.float32)
    membrane = jnp.zeros((member_count, EPIS, NEUR), jnp.float32)
    spikes = jnp.zeros((member_count, EPIS, NEUR), jnp.bfloat16)
    readout_sum = jnp.zeros((member_count, EPIS), jnp.float32)
    for moment in range(STEPS):
        current = jnp.broadcast_to(input_drive[moment][None], membrane.shape)
        if moment > 0:
            recurrent = jnp.dot(spikes.reshape(member_count * EPIS, NEUR), w_rec, preferred_element_type=jnp.float32)
            projection = jnp.einsum('men,mn->me', spikes.astype(jnp.float32), pre_side.astype(jnp.float32), precision=lax.Precision.HIGHEST)
            current = current + recurrent.reshape(member_count, EPIS, NEUR) + sigma_scale * projection[:, :, None] * post_side[:, None, :]
        membrane = leak_rate * (membrane - spikes.astype(jnp.float32)) + current
        spikes = jax.nn.sigmoid(4.0 * (membrane - 1.0)).astype(jnp.bfloat16)
        readout_sum = readout_sum + jnp.einsum('men,n->me', spikes.astype(jnp.float32), readout, precision=lax.Precision.HIGHEST)
    returns = lax.optimization_barrier(jnp.sum(readout_sum, axis=1)) / (EPIS * STEPS)
    fitness = member_ranks.astype(jnp.float32) / (member_count - 1) - 0.5 + returns
    weighted = pre_side.astype(jnp.float32) * fitness[:, None]
    grad_rec = jnp.dot(weighted.T, post_side, precision=lax.Precision.HIGHEST) * jnp.sqrt(12.0 / member_count)
    return (returns, grad_rec.astype(jnp.bfloat16))
```

```python
import jax
import jax.numpy as jnp
from jax import lax
from jax.sharding import PartitionSpec as P

sigma_scale = 0.01
f32 = jnp.float32
bf16 = jnp.bfloat16


def spike(membrane):
    return jax.nn.sigmoid(4.0 * (membrane - 1.0)).astype(bf16)


def swap(x, axis, mask):
    return lax.ppermute(x, axis, [(i, i ^ mask) for i in range(lax.axis_size(axis))])


def chip_blocks(x):
    chips = lax.axis_size("tp") // 2
    chip = lax.axis_index("tp") // 2
    if chips != 4:
        groups = [[2 * q + c for q in range(chips)] for c in range(2)]
        every = lax.all_gather(x, "tp", axis_index_groups=groups)
        return [(every[q], jnp.int32(q)) for q in range(chips)]
    half = x.shape[1] // 2
    over_x = swap(x, "tp", 2)
    over_y = swap(x, "tp", 4)
    left = swap(over_x[:, :half], "tp", 4)
    right = swap(over_y[:, half:], "tp", 2)
    return [(x, chip), (over_x, chip ^ 1), (over_y, chip ^ 2), (jnp.concatenate([left, right], 1), chip ^ 3)]


def shards(
    in_spikes, w_in, w_rec, leak_rate, neuron_bias, readout, pert_table, pert_idx, member_ranks
):
    steps, epis, inputs = in_spikes.shape
    members = pert_idx.shape[0]
    half = members // 2
    width = w_rec.shape[1]
    tp, pop = lax.axis_size("tp"), lax.axis_size("pop")
    me, plane = lax.axis_index("tp"), lax.axis_index("pop")
    chip, core = me // 2, me % 2
    member_count = members * pop
    epad = -(-epis // 16) * 16

    w_sib = swap(w_rec, "tp", 1)
    spike_input = in_spikes.astype(bf16).reshape(steps * epis, inputs)
    drive = (jnp.dot(spike_input, w_in, preferred_element_type=f32) + neuron_bias).reshape(steps, epis, width)
    s0 = spike(drive[0])
    side = jnp.concatenate([drive.reshape(steps * epis, width), leak_rate[None], readout[None]], 0)
    side_sib = swap(side, "tp", 1)
    pre_loc = jnp.take(pert_table, pert_idx[:, 0], axis=0)
    post_loc = jnp.take(pert_table, pert_idx[:, 1], axis=0)
    s0p = jnp.pad(s0, ((0, epad - epis), (0, 0)))
    load = jnp.stack(
        [jnp.concatenate([s0p, pre_loc[c * half:(c + 1) * half], post_loc[c * half:(c + 1) * half]], 0) for c in range(2)]
    )
    load = jnp.broadcast_to(load[None], (tp // 2,) + load.shape).reshape((tp,) + load.shape[1:])
    got = lax.all_to_all(load, "tp", 0, 0)
    s0_full, pre_full, post_full = got[:, :epis], got[:, epad:epad + half], got[:, epad + half:]
    w_own = w_rec.reshape(tp, width, width)
    base = leak_rate * (drive[0] - s0.astype(f32)) + drive[1] + jnp.einsum("jek,jkn->en", s0_full, w_own, preferred_element_type=f32)
    proj1 = jnp.einsum("jek,jmk->em", s0_full, pre_full, preferred_element_type=f32)
    base_full = lax.all_to_all(jnp.broadcast_to(base[None], (tp,) + base.shape), "tp", 0, 0)
    mem1 = base_full[:, :, None, :] + sigma_scale * proj1[None, :, :, None] * post_full.astype(f32)[:, None, :, :]
    s1 = spike(mem1)
    rows = epis * half
    proj2 = jnp.einsum("jemk,jmk->em", s1.astype(f32), pre_full.astype(f32))
    s1f = s1.reshape(tp, rows, width)
    is_low = core == 0

    def pair(own, sib, axis):
        return jnp.concatenate([jnp.where(is_low, own, sib), jnp.where(is_low, sib, own)], axis)

    sides = pair(side, side_sib, 1)
    drives = sides[: steps * epis].reshape(steps, epis, 1, 2 * width)
    leak, read = sides[steps * epis], sides[steps * epis + 1]
    w2 = pair(w_rec, w_sib, 1)

    def chip_cols(x):
        two = lax.dynamic_slice_in_dim(x, chip * 2, 2, 0)
        return jnp.concatenate([two[0], two[1]], -1)

    post = chip_cols(post_full).astype(f32)[None]
    s1c = chip_cols(s1).astype(f32)
    m1c = chip_cols(mem1)
    rec = jnp.einsum("jrk,jkn->rn", s1f, w2.reshape(tp, width, 2 * width), preferred_element_type=f32)
    mem2 = leak * (m1c - s1c) + drives[2] + rec.reshape(epis, half, 2 * width) + sigma_scale * proj2[:, :, None] * post
    s2 = spike(mem2)
    blocks = chip_blocks(s2.reshape(rows, 2 * width))
    pre_z = [pre_full] + [swap(pre_full, "pop", s) for s in range(1, pop)]
    post_z = [post_loc] + [swap(post_loc, "pop", s) for s in range(1, pop)]
    pre_own = jnp.stack(pre_z).transpose(0, 2, 1, 3).reshape(pop * half, inputs)
    pre_oth = swap(pre_own, "tp", 1)
    pre_all = pair(pre_own.reshape(pop, half, inputs), pre_oth.reshape(pop, half, inputs), 1).reshape(member_count, inputs)
    post_all = jnp.stack(post_z).reshape(member_count, width)

    mem3 = leak * (mem2 - s2.astype(f32)) + drives[3]
    proj3 = 0.0
    pre_w = pre_full.transpose(1, 0, 2).reshape(half, inputs)
    for block, q in blocks:
        wq = lax.dynamic_slice_in_dim(w2, q * 2 * width, 2 * width, 0)
        pq = lax.dynamic_slice_in_dim(pre_w, q * 2 * width, 2 * width, 1)
        mem3 = mem3 + jnp.dot(block, wq, preferred_element_type=f32).reshape(mem3.shape)
        proj3 = proj3 + jnp.einsum("emk,mk->em", block.reshape(epis, half, 2 * width).astype(f32), pq.astype(f32))
    mem3 = mem3 + sigma_scale * proj3[:, :, None] * post
    s3 = spike(mem3)
    s0c = chip_cols(s0_full).astype(f32)
    total = (
        jnp.sum(s0c * read)
        + jnp.sum((s1c + s2.astype(f32) + s3.astype(f32)) * read, axis=(0, 2))
    )
    ranks = lax.dynamic_slice_in_dim(member_ranks, core * half, half, 0).astype(f32)
    note = jnp.stack([total, ranks])
    notes = lax.all_to_all(jnp.broadcast_to(note[None], (pop * tp,) + note.shape), ("pop", "tp"), 0, 0)
    notes = notes.reshape(pop, tp // 2, 2, 2, half)
    returns = jnp.sum(notes[:, :, :, 0], axis=1).reshape(pop, members) / (epis * steps)
    ranks_all = notes[:, 0, :, 1].reshape(pop, members)
    fitness = ranks_all / (member_count - 1) - 0.5 + returns
    order = plane ^ jnp.arange(pop)
    scale = (jnp.take(fitness, order, axis=0) * jnp.sqrt(12.0 / member_count)).reshape(member_count, 1)
    weighted = post_all.astype(f32) * scale
    high = weighted.astype(bf16)
    low = (weighted - high.astype(f32)).astype(bf16)
    both = jnp.concatenate([high, low], 0)
    pre_two = jnp.concatenate([pre_all, pre_all], 0)
    grad = lax.dot_general(pre_two, both, (((0,), (0,)), ((), ())), preferred_element_type=f32).astype(bf16)
    mine = lax.dynamic_slice_in_dim(returns, plane, 1, 0)[0]
    return (mine, grad)


def solution(mesh):
    placed = (
        P(),
        P(None, "tp"),
        P(None, "tp"),
        P("tp"),
        P("tp"),
        P("tp"),
        P(None, "tp"),
        P("pop", None),
        P("pop"),
    )
    return jax.shard_map(
        shards, mesh=mesh, in_specs=placed, out_specs=(P("pop"), P(None, "tp")), check_vma=False
    )
```

```python
import functools

import jax
import jax.numpy as jnp
from jax import lax
from jax.experimental import pallas as pl
from jax.experimental.pallas import tpu as pltpu
from jax.sharding import PartitionSpec as P

sigma_scale = 0.01
f32 = jnp.float32
bf16 = jnp.bfloat16
i32 = jnp.int32
EP = 16
VMEM_LIMIT = 24 * 2**20


def spike(membrane):
    return (0.5 + 0.5 * jnp.tanh(2.0 * (membrane - 1.0))).astype(bf16)


def dot(a, b):
    return jnp.dot(a, b, preferred_element_type=f32)


def fold(x):
    parts = [x[:, i : i + 128] for i in range(0, x.shape[1], 128)]
    return functools.reduce(jnp.add, parts)


def params(cost_flops, cost_bytes):
    return dict(
        compiler_params=pltpu.CompilerParams(vmem_limit_bytes=VMEM_LIMIT, dimension_semantics=("arbitrary",)),
        cost_estimate=pl.CostEstimate(flops=cost_flops, bytes_accessed=cost_bytes, transcendentals=0),
    )


def whole(shape):
    return pl.BlockSpec(shape, lambda *_: (0,) * len(shape))


def drive_kernel(spk_ref, win_ref, bias_ref, leak_ref, read_ref, table_ref, idx_ref, side_ref, load_ref, post_ref, acc_ref):
    k = pl.program_id(0)
    steps, epis, depth = spk_ref.shape
    tp = load_ref.shape[0]

    @pl.when(k == 0)
    def _():
        acc_ref[...] = jnp.zeros_like(acc_ref)
        count = idx_ref.shape[0]
        at = lax.broadcasted_iota(i32, (count, table_ref.shape[0]), 1)
        pre_hot = jnp.where(at == idx_ref[:, 0:1], 1.0, 0.0).astype(bf16)
        post_hot = jnp.where(at == idx_ref[:, 1:2], 1.0, 0.0).astype(bf16)
        pre = dot(pre_hot, table_ref[...]).astype(bf16)
        post = dot(post_hot, table_ref[...]).astype(bf16)
        for j in range(tp):
            c = j % 2
            load_ref[j, EP : 2 * EP, :] = pre[c * EP : (c + 1) * EP]
            load_ref[j, 2 * EP : 3 * EP, :] = post[c * EP : (c + 1) * EP]
        for c in range(2):
            post_ref[c] = post[c * EP : (c + 1) * EP]

    blank = jnp.zeros((EP - epis, depth), i32)
    rows = [jnp.concatenate([spk_ref[t], blank], 0).astype(f32).astype(bf16) for t in range(steps)]
    acc_ref[...] += dot(jnp.concatenate(rows, 0), win_ref[...])

    @pl.when(k == pl.num_programs(0) - 1)
    def _():
        drive = acc_ref[...] + bias_ref[...]
        side_ref[: steps * EP, :] = drive
        row = lax.broadcasted_iota(i32, (8, drive.shape[1]), 0)
        side_ref[steps * EP :, :] = jnp.where(row == 0, leak_ref[...], read_ref[...])
        s0 = spike(drive[:EP]).astype(f32)
        here = lax.broadcasted_iota(i32, s0.shape, 0) < epis
        s0 = jnp.where(here, s0, 0.0).astype(bf16)
        for j in range(tp):
            load_ref[j, 0:EP, :] = s0


def drive_call(in_spikes, w_in, bias, leak, read, table, idx, tp):
    steps, epis, inputs = in_spikes.shape
    width = w_in.shape[1]
    depth = min(1024, inputs)
    members = idx.shape[0]
    rows = steps * EP
    return pl.pallas_call(
        drive_kernel,
        grid=(inputs // depth,),
        in_specs=[
            pl.BlockSpec((steps, epis, depth), lambda k: (0, 0, k)),
            pl.BlockSpec((depth, width), lambda k: (k, 0)),
            whole((1, width)),
            whole((1, width)),
            whole((1, width)),
            whole(table.shape),
            whole((members, 2)),
        ],
        out_specs=[whole((rows + 8, width)), whole((tp, 3 * EP, width)), whole((2, EP, width))],
        out_shape=[
            jax.ShapeDtypeStruct((rows + 8, width), f32),
            jax.ShapeDtypeStruct((tp, 3 * EP, width), bf16),
            jax.ShapeDtypeStruct((2, EP, width), bf16),
        ],
        scratch_shapes=[pltpu.VMEM((rows, width), f32)],
        name="drive",
        **params(2 * rows * inputs * width, inputs * width * 2 + steps * 16 * inputs * 4),
    )(in_spikes, w_in, bias, leak, read, table, idx)


def base_kernel(s0_ref, pre_ref, w_ref, side_ref, out_ref, proj_ref, acc_ref):
    j = pl.program_id(0)
    steps_rows = side_ref.shape[0] - 8

    @pl.when(j == 0)
    def _():
        acc_ref[...] = jnp.zeros_like(acc_ref)
        proj_ref[...] = jnp.zeros_like(proj_ref)

    s0 = s0_ref[0]
    acc_ref[...] += dot(s0, w_ref[...])
    proj_ref[...] += lax.dot_general(pre_ref[0], s0, (((1,), (1,)), ((), ())), preferred_element_type=f32)

    @pl.when(j == pl.num_programs(0) - 1)
    def _():
        mem0 = side_ref[0:EP, :]
        leak = side_ref[steps_rows : steps_rows + 1, :]
        base = leak * (mem0 - spike(mem0).astype(f32)) + side_ref[EP : 2 * EP, :] + acc_ref[...]
        for i in range(out_ref.shape[0]):
            out_ref[i] = base


def base_call(got, w_rec, side):
    tp, _, width = got.shape
    return pl.pallas_call(
        base_kernel,
        grid=(tp,),
        in_specs=[
            pl.BlockSpec((1, EP, width), lambda j: (j, 0, 0)),
            pl.BlockSpec((1, EP, width), lambda j: (j, 1, 0)),
            pl.BlockSpec((width, width), lambda j: (j, 0)),
            whole(side.shape),
        ],
        out_specs=[whole((tp, EP, width)), whole((EP, EP))],
        out_shape=[jax.ShapeDtypeStruct((tp, EP, width), f32), jax.ShapeDtypeStruct((EP, EP), f32)],
        scratch_shapes=[pltpu.VMEM((EP, width), f32)],
        name="base",
        **params(2 * EP * tp * width * width, tp * width * width * 2),
    )(got, got, w_rec, side)


def step2_kernel(
    me_ref, base_ref, s0_ref, pre_ref, post_ref, wo_ref, ws_ref, proj1_ref, so_ref, ss_ref,
    s2o_ref, s2s_ref, nexto_ref, nexts_ref, postc_ref, read_ref,
    s1_ref, acco_ref, accs_ref, carry_ref, p2_ref, rs_ref, *, epis,
):
    j = pl.program_id(0)
    width = base_ref.shape[2]
    lead = so_ref.shape[0] - 8

    def membrane1(e):
        c = sigma_scale * proj1_ref[:, e : e + 1]
        return base_ref[0, e : e + 1, :] + c * post_ref[0].astype(f32)

    @pl.when(j == 0)
    def _():
        acco_ref[...] = jnp.zeros_like(acco_ref)
        accs_ref[...] = jnp.zeros_like(accs_ref)
        p2_ref[...] = jnp.zeros_like(p2_ref)
        rs_ref[...] = jnp.zeros_like(rs_ref)

    pre = pre_ref[0].astype(f32)
    for e in range(epis):
        at = slice(e * EP, (e + 1) * EP)
        s1 = spike(membrane1(e))
        s1_ref[at, :] = s1
        p2_ref[at, :] += fold(s1.astype(f32) * pre)

    def chip_part(h, side_ref):
        leak, read = side_ref[lead : lead + 1, :], side_ref[lead + 1 : lead + 2, :]
        postc_ref[h] = post_ref[0]
        s0 = s0_ref[0].astype(f32)
        total = jnp.broadcast_to(jnp.sum(s0, 0, keepdims=True), (EP, width))
        for e in range(epis):
            at = slice(e * EP, (e + 1) * EP)
            s1 = s1_ref[at, :].astype(f32)
            total += s1
            carry_ref[h, at, :] = leak * (membrane1(e) - s1) + side_ref[2 * EP + e : 2 * EP + e + 1, :]
        rs_ref[...] += fold(total * read)

    @pl.when(j == 0)
    def _():
        chip_part(0, so_ref)

    @pl.when(j == 1)
    def _():
        chip_part(1, ss_ref)

    acco_ref[...] += dot(s1_ref[...], wo_ref[...])
    accs_ref[...] += dot(s1_ref[...], ws_ref[...])

    @pl.when(j == pl.num_programs(0) - 1)
    def _():
        proj2 = sigma_scale * jnp.sum(p2_ref[...], axis=1, keepdims=True)
        for h, side_ref, acc_ref, s2_ref, next_ref in (
            (0, so_ref, acco_ref, s2o_ref, nexto_ref),
            (1, ss_ref, accs_ref, s2s_ref, nexts_ref),
        ):
            leak, read = side_ref[lead : lead + 1, :], side_ref[lead + 1 : lead + 2, :]
            post = postc_ref[h].astype(f32)
            total = jnp.zeros((EP, width), f32)
            for e in range(epis):
                at = slice(e * EP, (e + 1) * EP)
                mem = carry_ref[h, at, :] + acc_ref[at, :] + proj2[at, :] * post
                s2 = spike(mem)
                s2_ref[at, :] = s2
                s2 = s2.astype(f32)
                total += s2
                next_ref[at, :] = leak * (mem - s2) + side_ref[3 * EP + e : 3 * EP + e + 1, :]
            rs_ref[...] += fold(total * read)
        read_ref[...] = rs_ref[...]


def step2_call(me, base, got, w_rec, w_sib, proj1, side, side_sib, epis):
    tp, _, width = got.shape
    rows = epis * EP
    far = lambda block: pl.BlockSpec((1, EP, width), lambda j, me: (j ^ me[0], block, 0))
    weight = pl.BlockSpec((width, width), lambda j, me: (j ^ me[0], 0))
    spec = pltpu.PrefetchScalarGridSpec(
        num_scalar_prefetch=1,
        grid=(tp,),
        in_specs=[far(0), far(0), far(1), far(2), weight, weight, whole((EP, EP)), whole(side.shape), whole(side.shape)],
        out_specs=[whole((rows, width))] * 4 + [whole((2, EP, width)), whole((EP, 128))],
        scratch_shapes=[
            pltpu.VMEM((rows, width), bf16),
            pltpu.VMEM((rows, width), f32),
            pltpu.VMEM((rows, width), f32),
            pltpu.VMEM((2, rows, width), f32),
            pltpu.VMEM((rows, 128), f32),
            pltpu.VMEM((EP, 128), f32),
        ],
    )
    sds = jax.ShapeDtypeStruct
    return pl.pallas_call(
        functools.partial(step2_kernel, epis=epis),
        grid_spec=spec,
        out_shape=[
            sds((rows, width), bf16), sds((rows, width), bf16), sds((rows, width), f32), sds((rows, width), f32),
            sds((2, EP, width), bf16), sds((EP, 128), f32),
        ],
        name="step2",
        **params(4 * rows * tp * width * width, 4 * tp * width * width),
    )(me, base, got, got, got, w_rec, w_sib, proj1, side, side_sib)


def accumulate(j, blocks, wo_ref, ws_ref, pre_ref, acco_ref, accs_ref, p_ref):
    for n, block_ref in enumerate(blocks):

        @pl.when(j == n)
        def _(block_ref=block_ref):
            acco_ref[...] += dot(block_ref[...], wo_ref[...])
            accs_ref[...] += dot(block_ref[...], ws_ref[...])
            pre = pre_ref[0].astype(f32)
            for r in range(0, block_ref.shape[0], EP):
                p_ref[r : r + EP, :] += fold(block_ref[r : r + EP, :].astype(f32) * pre)


def part_kernel(me_ref, *refs, count, first, packs):
    blocks, refs = refs[:count], refs[count:]
    wo_ref, ws_ref, pre_ref, acco_in, accs_in, p_in = refs[:6]
    rest = refs[6:]
    j = pl.program_id(0)
    if packs:
        got_ref, post_ref, acco_ref, accs_ref, p_ref, pack_ref = rest
    else:
        acco_ref, accs_ref, p_ref = rest

    @pl.when(j == 0)
    def _():
        acco_ref[...] = acco_in[...]
        accs_ref[...] = accs_in[...]
        p_ref[...] = jnp.zeros_like(p_ref) if first else p_in[...]
        if packs:
            tp = got_ref.shape[0]
            for i in range(tp):
                pack_ref[i] = got_ref[i]
            for c in range(2):
                pack_ref[tp + c] = post_ref[c]

    accumulate(j, blocks, wo_ref, ws_ref, pre_ref, acco_ref, accs_ref, p_ref)


def table_index(order):
    def of(j):
        at = jnp.int32(order[0])
        for n, v in enumerate(order[1:], 1):
            at = jnp.where(j == n, jnp.int32(v), at)
        return at

    return of


def part_specs(blocks, order, got, shapes):
    rows, width = blocks[0].shape
    at = table_index(order)
    weight = pl.BlockSpec((width, width), lambda j, me: (at(j) ^ me[0], 0))
    return [whole((rows, width)) for _ in blocks] + [
        weight,
        weight,
        pl.BlockSpec((1, EP, width), lambda j, me: (at(j) ^ me[0], 1, 0)),
    ] + [whole(s) for s in shapes]


def part_call(me, blocks, order, w_rec, w_sib, got, acco, accs, proj, post_loc=None):
    rows, width = blocks[0].shape
    tp = got.shape[0]
    first = proj is None
    packs = post_loc is not None
    if first:
        proj = jnp.zeros((EP, 128), f32)
    ins = part_specs(blocks, order, got, [(rows, width), (rows, width), proj.shape])
    sds = jax.ShapeDtypeStruct
    outs = [sds((rows, width), f32), sds((rows, width), f32), sds((rows, 128), f32)]
    args = [me, *blocks, w_rec, w_sib, got, acco, accs, proj]
    if packs:
        ins += [pl.BlockSpec((tp, EP, width), lambda j, me: (0, 1, 0)), whole(post_loc.shape)]
        outs += [sds((tp + 2, EP, width), bf16)]
        args += [got, post_loc]
    spec = pltpu.PrefetchScalarGridSpec(
        num_scalar_prefetch=1,
        grid=(len(blocks),),
        in_specs=ins,
        out_specs=[whole(o.shape) for o in outs],
    )
    n = len(blocks)
    return pl.pallas_call(
        functools.partial(part_kernel, count=n, first=first, packs=packs),
        grid_spec=spec,
        out_shape=outs,
        name="part",
        **params(4 * rows * n * width * width, 4 * n * width * width + 16 * rows * width),
    )(*args)


def last_kernel(me_ref, *refs, count, epis, copies):
    blocks, refs = refs[:count], refs[count:]
    wo_ref, ws_ref, pre_ref, acco_in, accs_in, p_in, so_ref, ss_ref, postc_ref, read_ref, ranks_ref = refs[:11]
    note_ref, acco_ref, accs_ref, p_ref = refs[11:]
    j = pl.program_id(0)
    lead = so_ref.shape[0] - 8

    @pl.when(j == 0)
    def _():
        acco_ref[...] = acco_in[...]
        accs_ref[...] = accs_in[...]
        p_ref[...] = p_in[...]

    accumulate(j, blocks, wo_ref, ws_ref, pre_ref, acco_ref, accs_ref, p_ref)

    @pl.when(j == pl.num_programs(0) - 1)
    def _():
        proj = sigma_scale * jnp.sum(p_ref[...], axis=1, keepdims=True)
        sums = read_ref[...]
        for h, side_ref, acc_ref in ((0, so_ref, acco_ref), (1, ss_ref, accs_ref)):
            read = side_ref[lead + 1 : lead + 2, :]
            post = postc_ref[h].astype(f32)
            total = jnp.zeros(post.shape, f32)
            for e in range(epis):
                at = slice(e * EP, (e + 1) * EP)
                total += spike(acc_ref[at, :] + proj[at, :] * post).astype(f32)
            sums += fold(total * read)
        sums = jnp.sum(sums, axis=1, keepdims=True)
        row = lax.broadcasted_iota(i32, (EP, 128), 0)
        lane = lax.broadcasted_iota(i32, (EP, 128), 1) & (EP - 1)
        flat = jnp.sum(jnp.where(row == lane, sums, 0.0), axis=0, keepdims=True)
        core = me_ref[0] & 1
        ranks = ranks_ref[...].astype(f32)
        mine = jnp.where(core == 0, ranks[:EP], ranks[EP:])
        rank = jnp.sum(jnp.where(row == lane, mine, 0.0), axis=0, keepdims=True)
        odd = (lax.broadcasted_iota(i32, (2 * copies, 128), 0) & 1) == 1
        note_ref[...] = jnp.where(odd, rank, flat)


def last_call(me, blocks, order, w_rec, w_sib, got, acco, accs, proj, side, side_sib, postc, read, ranks, epis, copies):
    rows, width = blocks[0].shape
    ins = part_specs(
        blocks, order, got,
        [(rows, width), (rows, width), proj.shape, side.shape, side.shape, postc.shape, read.shape, ranks.shape],
    )
    spec = pltpu.PrefetchScalarGridSpec(
        num_scalar_prefetch=1,
        grid=(len(blocks),),
        in_specs=ins,
        out_specs=whole((2 * copies, 128)),
        scratch_shapes=[
            pltpu.VMEM((rows, width), f32),
            pltpu.VMEM((rows, width), f32),
            pltpu.VMEM((rows, 128), f32),
        ],
    )
    n = len(blocks)
    return pl.pallas_call(
        functools.partial(last_kernel, count=n, epis=epis, copies=copies),
        grid_spec=spec,
        out_shape=jax.ShapeDtypeStruct((2 * copies, 128), f32),
        name="last",
        **params(4 * rows * n * width * width, 4 * n * width * width + 16 * rows * width),
    )(me, *blocks, w_rec, w_sib, got, acco, accs, proj, side, side_sib, postc, read, ranks)


def prep_kernel(*refs, pop):
    packs, (pret_ref, post_ref) = refs[: 2 * pop], refs[2 * pop :]
    tp = packs[0].shape[0] - 2
    width = packs[0].shape[2]
    own = packs[:pop]
    for b in range(tp):
        cols = jnp.concatenate([p[b] for p in packs], 0)
        pret_ref[b * width : (b + 1) * width, :] = cols.astype(f32).T.astype(bf16)
    return own, post_ref


def prep_full_kernel(core_ref, *refs, pop):
    own, post_ref = prep_kernel(*refs, pop=pop)
    tp = own[0].shape[0] - 2
    core = core_ref[0]
    for d in range(2):
        for s in range(pop):
            at = (d * pop + s) * EP
            low, high = own[s][tp + d], own[s][tp + 1 - d]
            post_ref[at : at + EP, :] = jnp.where(core == 0, low.astype(f32), high.astype(f32)).astype(bf16)


def prep_call(core, packs, pop):
    blocks, _, width = packs[0].shape
    count = 2 * pop * EP
    sds = jax.ShapeDtypeStruct
    outs = [sds(((blocks - 2) * width, count), bf16), sds((count, width), bf16)]
    return pl.pallas_call(
        functools.partial(prep_full_kernel, pop=pop),
        grid_spec=pltpu.PrefetchScalarGridSpec(
            num_scalar_prefetch=1,
            grid=(1,),
            in_specs=[whole(p.shape) for p in packs],
            out_specs=[whole(o.shape) for o in outs],
        ),
        out_shape=outs,
        name="prep",
        **params(count * blocks * width, 4 * count * blocks * width),
    )(core, *packs)


def grad_kernel(place_ref, note_ref, pret_ref, post_ref, grad_ref, ret_ref, both_ref, *, tp, pop, plays):
    count = post_ref.shape[0]
    plane, core = place_ref[0], place_ref[1]

    @pl.when(pl.program_id(0) == 0)
    def _():
        notes = note_ref[...]
        wide = jnp.concatenate([notes] * (count // 128), 1) if count > 128 else notes
        row = lax.broadcasted_iota(i32, wide.shape, 0)
        lane = lax.broadcasted_iota(i32, wide.shape, 1)
        source = row >> 1
        kind = row & 1
        place = source // tp if tp & (tp - 1) else source >> (tp.bit_length() - 1)
        unit = source & 1
        group = lane >> 4
        want_plane = plane ^ (group & (pop - 1))
        want_core = core ^ (group >> (pop.bit_length() - 1))
        match = (place == want_plane) & (unit == want_core)
        total = jnp.sum(jnp.where(match & (kind == 0), wide, 0.0), 0, keepdims=True)
        lead = (source & (tp - 1)) < 2
        rank = jnp.sum(jnp.where(match & (kind == 1) & lead, wide, 0.0), 0, keepdims=True)
        fitness = rank / (count - 1) - 0.5 + total / plays
        fitness = fitness * ((12.0 / count) ** 0.5)
        diag = lax.broadcasted_iota(i32, (count, count), 0) == lax.broadcasted_iota(i32, (count, count), 1)
        column = jnp.sum(jnp.where(diag, fitness, 0.0), 1, keepdims=True)
        weighted = post_ref[...].astype(f32) * column
        high = weighted.astype(bf16)
        both_ref[:count, :] = high
        both_ref[count:, :] = (weighted - high.astype(f32)).astype(bf16)
        row = lax.broadcasted_iota(i32, notes.shape, 0)
        lane = lax.broadcasted_iota(i32, notes.shape, 1)
        source = row >> 1
        place = source >> (tp.bit_length() - 1)
        mine = (place == plane) & ((source & 1) == (lane >> 4)) & ((row & 1) == 0)
        ret_ref[...] = jnp.sum(jnp.where(mine, notes, 0.0), 0, keepdims=True) / plays

    pret = pret_ref[...]
    grad_ref[...] = dot(jnp.concatenate([pret, pret], 1), both_ref[...]).astype(bf16)


def grad_call(place, notes, pret, post, tp, pop, plays):
    inputs, count = pret.shape
    width = post.shape[1]
    block = min(512, inputs)
    return pl.pallas_call(
        functools.partial(grad_kernel, tp=tp, pop=pop, plays=plays),
        grid_spec=pltpu.PrefetchScalarGridSpec(
            num_scalar_prefetch=1,
            grid=(inputs // block,),
            in_specs=[whole(notes.shape), pl.BlockSpec((block, count), lambda i, _: (i, 0)), whole(post.shape)],
            out_specs=[pl.BlockSpec((block, width), lambda i, _: (i, 0)), whole((1, 128))],
            scratch_shapes=[pltpu.VMEM((2 * count, width), bf16)],
        ),
        out_shape=[jax.ShapeDtypeStruct((inputs, width), bf16), jax.ShapeDtypeStruct((1, 128), f32)],
        name="grad",
        **params(4 * inputs * count * width, 2 * inputs * (count + width)),
    )(place, notes, pret, post)


def swap(x, axis, mask):
    return lax.ppermute(x, axis, [(i, i ^ mask) for i in range(lax.axis_size(axis))])


def shards(
    in_spikes, w_in, w_rec, leak_rate, neuron_bias, readout, pert_table, pert_idx, member_ranks
):
    steps, epis, inputs = in_spikes.shape
    members = pert_idx.shape[0]
    tp, pop = lax.axis_size("tp"), lax.axis_size("pop")
    assert steps == 4 and epis < EP and members == 2 * EP
    me, plane = lax.axis_index("tp"), lax.axis_index("pop")
    at = me[None].astype(i32)
    place = jnp.stack([plane, me & 1]).astype(i32)

    w_sib = swap(w_rec, "tp", 1)
    side, load, post_loc = drive_call(
        in_spikes, w_in, neuron_bias[None], leak_rate[None], readout[None], pert_table, pert_idx, tp
    )
    side_sib = swap(side, "tp", 1)
    got = lax.all_to_all(load, "tp", 0, 0)
    base_out, proj1 = base_call(got, w_rec, side)
    base = lax.all_to_all(base_out, "tp", 0, 0)
    s2o, s2s, acco, accs, postc, read = step2_call(at, base, got, w_rec, w_sib, proj1, side, side_sib, epis)

    far, order = [], []
    if tp == 8:
        xa, yb = swap(s2o, "tp", 2), swap(s2s, "tp", 4)
        xb, ya = swap(s2s, "tp", 2), swap(s2o, "tp", 4)
        far, order = [xa, yb, xb, ya], [2, 5, 3, 4]
        end, end_order = [swap(xa, "tp", 4), swap(yb, "tp", 2)], [6, 7]
    else:
        for mask in range(2, tp, 2):
            far += [swap(s2o, "tp", mask), swap(s2s, "tp", mask)]
            order += [mask, mask + 1]
        far, end, order, end_order = far[:-2], far[-2:], order[:-2], order[-2:]
    acco, accs, proj, pack = part_call(at, [s2o, s2s], [0, 1], w_rec, w_sib, got, acco, accs, None, post_loc)
    packs = [pack] + [swap(pack, "pop", s) for s in range(1, pop)]
    packs += [swap(p, "tp", 1) for p in packs]
    acco, accs, proj = part_call(at, far, order, w_rec, w_sib, got, acco, accs, proj)
    notes = last_call(
        at, end, end_order, w_rec, w_sib, got, acco, accs, proj, side, side_sib, postc, read,
        member_ranks[:, None], epis, pop * tp,
    )
    notes = lax.all_to_all(notes, ("pop", "tp"), 0, 0, tiled=True)
    pret, post_all = prep_call(place[1:], packs, pop)
    grad, returns = grad_call(place, notes, pret, post_all, tp, pop, epis * steps)
    return (returns[0, :members], grad)


def solution(mesh):
    placed = (
        P(),
        P(None, "tp"),
        P(None, "tp"),
        P("tp"),
        P("tp"),
        P("tp"),
        P(None, "tp"),
        P("pop", None),
        P("pop"),
    )
    return jax.shard_map(
        shards, mesh=mesh, in_specs=placed, out_specs=(P("pop"), P(None, "tp")), check_vma=False
    )
```

```python
import functools

import jax
import jax.numpy as jnp
from jax import lax
from jax.experimental import pallas as pl
from jax.experimental.pallas import tpu as pltpu
from jax.sharding import PartitionSpec as P

sigma_scale = 0.01
f32 = jnp.float32
bf16 = jnp.bfloat16
i32 = jnp.int32
L_BASE = 48
L_STEP2 = 32
L_PART = 24
L_DRIVE = 58
L_LAST = 24
EP = 16


def spike(membrane):
    return (0.5 + 0.5 * jnp.tanh(2.0 * (membrane - 1.0))).astype(bf16)


def dot(a, b):
    return jnp.dot(a, b, preferred_element_type=f32)


def fold(x):
    parts = [x[:, i : i + 128] for i in range(0, x.shape[1], 128)]
    return functools.reduce(jnp.add, parts)


def params(mib, flops, nbytes):
    return dict(
        compiler_params=pltpu.CompilerParams(vmem_limit_bytes=mib * 2**20),
        cost_estimate=pl.CostEstimate(flops=flops, bytes_accessed=nbytes, transcendentals=0),
    )


VM = pl.BlockSpec(memory_space=pltpu.VMEM)
SM = pl.BlockSpec(memory_space=pltpu.SMEM)
HB = pl.BlockSpec(memory_space=pltpu.HBM)
sds = jax.ShapeDtypeStruct


def block_rows(b, width):
    return pl.ds(pl.multiple_of(b * width, width), width)


def drive_kernel(
    spk_hbm, win_hbm, bias_hbm, leak_hbm, read_hbm, table_hbm, idx_hbm,
    side_ref, load_ref, post_ref,
    spk, win, bias, leak, read, table, idx, acc_ref, sems,
):
    epis, steps, inputs = spk.shape
    tp = load_ref.shape[0]
    parts = 4
    depth = inputs // parts
    copies = []
    for k in range(parts):
        at = pl.ds(k * depth, depth)
        copies.append((spk_hbm.at[:, :, at], spk.at[:, :, at]))
        copies.append((win_hbm.at[at], win.at[at]))
    copies += [(table_hbm, table), (idx_hbm, idx), (bias_hbm, bias), (leak_hbm, leak), (read_hbm, read)]
    copies = [pltpu.make_async_copy(a, b, sems.at[n]) for n, (a, b) in enumerate(copies)]
    for copy in copies:
        copy.start()
    for k in range(parts):
        copies[2 * k].wait()
        copies[2 * k + 1].wait()
        at = slice(k * depth, (k + 1) * depth)
        x = spk[:, :, at].reshape(epis * steps, depth).astype(f32).astype(bf16)
        part = dot(x, win[at, :])
        total = part if k == 0 else total + part
    for copy in copies[2 * parts :]:
        copy.wait()
    total = total + bias[...]
    lanes = range(acc_ref.shape[0])
    for c in lanes:
        acc_ref[c] = total[:, c * 128 : (c + 1) * 128]
    blank = jnp.zeros((EP - epis, total.shape[1]), f32)
    for t in range(steps):
        drive = jnp.concatenate([acc_ref[c, pl.ds(t, epis, stride=steps), :] for c in lanes], 1)
        drive = jnp.concatenate([drive, blank], 0)
        side_ref[t * EP : (t + 1) * EP, :] = drive
        if t == 0:
            s0 = spike(drive).astype(f32)
            here = lax.broadcasted_iota(i32, s0.shape, 0) < epis
            s0 = jnp.where(here, s0, 0.0).astype(bf16)
            for j in range(tp):
                load_ref[j, :EP, :] = s0
    row = lax.broadcasted_iota(i32, (8, total.shape[1]), 0)
    side_ref[steps * EP :, :] = jnp.where(row == 0, leak[...], read[...])
    at = lax.broadcasted_iota(i32, (table.shape[0], idx.shape[1]), 0)
    pick = (((0,), (0,)), ((), ()))
    pre, post = (
        lax.dot_general(
            jnp.where(at == idx[n : n + 1, :], 1.0, 0.0).astype(bf16), table[...], pick, preferred_element_type=f32
        ).astype(bf16)
        for n in range(2)
    )
    for j in range(tp):
        own = slice((j % 2) * EP, (j % 2 + 1) * EP)
        load_ref[j, EP : 2 * EP, :] = pre[own]
        load_ref[j, 2 * EP :, :] = post[own]
    for c in range(2):
        post_ref[c] = post[c * EP : (c + 1) * EP]


def drive_call(in_spikes, w_in, bias, leak, read, table, idx, tp):
    steps, epis, inputs = in_spikes.shape
    width = w_in.shape[1]
    members = idx.shape[0]
    ins = [in_spikes.transpose(1, 0, 2), w_in, bias[None], leak[None], read[None], table, idx.T]
    return pl.pallas_call(
        drive_kernel,
        in_specs=[HB] * 7,
        out_specs=[VM] * 3,
        out_shape=[
            sds((steps * EP + 8, width), f32),
            sds((tp, 3 * EP, width), bf16),
            sds((2, EP, width), bf16),
        ],
        scratch_shapes=[pltpu.VMEM(x.shape, x.dtype) for x in ins]
        + [pltpu.VMEM((width // 128, steps * epis, 128), f32), pltpu.SemaphoreType.DMA((13,))],
        name="drive",
        **params(L_DRIVE, 2 * steps * EP * inputs * width, inputs * width * 2 + steps * EP * inputs * 4),
    )(*ins)


def base_kernel(got_ref, w_hbm, side_ref, out_ref, w_ref, sems):
    tp, _, width = got_ref.shape
    lead = side_ref.shape[0] - 8
    parts = 4
    depth = w_ref.shape[0] // parts
    copies = []
    for k in range(parts):
        at = pl.ds(k * depth, depth)
        copies.append(pltpu.make_async_copy(w_hbm.at[at], w_ref.at[at], sems.at[k]))
    for copy in copies:
        copy.start()
    mem0 = side_ref[0:EP, :]
    leak = side_ref[lead : lead + 1, :]
    base = leak * (mem0 - spike(mem0).astype(f32)) + side_ref[EP : 2 * EP, :]
    for k in range(parts):
        copies[k].wait()
        for j in range(k * tp // parts, (k + 1) * tp // parts):
            base += dot(got_ref[j, :EP, :], w_ref[j * width : (j + 1) * width, :])
    for i in range(tp):
        out_ref[i] = base


def base_call(got, w_rec, side):
    tp, _, width = got.shape
    return pl.pallas_call(
        base_kernel,
        in_specs=[VM, HB, VM],
        out_specs=VM,
        out_shape=sds((tp, EP, width), f32),
        scratch_shapes=[pltpu.VMEM(w_rec.shape, bf16), pltpu.SemaphoreType.DMA((4,))],
        name="base",
        **params(L_BASE, 2 * EP * tp * width * width, tp * width * width * 2),
    )(got, w_rec, side)


def proj_kernel(got_ref, post_ref, proj_ref, pack_ref):
    tp = got_ref.shape[0]
    proj = jnp.zeros((EP, EP), f32)
    for j in range(tp):
        pre = got_ref[j, EP : 2 * EP, :]
        proj += lax.dot_general(pre, got_ref[j, :EP, :], (((1,), (1,)), ((), ())), preferred_element_type=f32)
        pack_ref[j] = pre
    proj_ref[...] = sigma_scale * proj
    for c in range(2):
        pack_ref[tp + c] = post_ref[c]


def proj_call(got, post_loc):
    tp, _, width = got.shape
    return pl.pallas_call(
        proj_kernel,
        in_specs=[VM] * 2,
        out_specs=[VM] * 2,
        out_shape=[sds((EP, EP), f32), sds((tp + 2, EP, width), bf16)],
        name="proj",
        **params(8, 2 * EP * EP * tp * width, 4 * tp * EP * width),
    )(got, post_loc)


def step2_kernel(
    me_ref, base_ref, rows_ref, wo_hbm, ws_hbm, proj1_ref, so_ref, ss_ref, near_ref,
    s2o_ref, s2s_ref, memo_ref, mems_ref, s1c_ref,
    s1_ref, wo_ref, ws_ref, acco_ref, accs_ref, p2_ref, sems, *, epis,
):
    tp, _, width = base_ref.shape
    lead = so_ref.shape[0] - 8
    me = me_ref[0]

    def fetch(j):
        at = block_rows(j ^ me, width)
        return (
            pltpu.make_async_copy(wo_hbm.at[at], wo_ref.at[at], sems.at[0, j]),
            pltpu.make_async_copy(ws_hbm.at[at], ws_ref.at[at], sems.at[1, j]),
        )

    for j in range(tp):
        for copy in fetch(j):
            copy.start()

    def membrane1(b, e, post):
        return base_ref[b, e : e + 1, :] + proj1_ref[:, e : e + 1] * post

    p2_ref[...] = jnp.zeros_like(p2_ref)
    acco_ref[...] = jnp.zeros_like(acco_ref)
    accs_ref[...] = jnp.zeros_like(accs_ref)

    def rebuild(j):
        b = j ^ me
        pre = rows_ref[b, EP : 2 * EP, :].astype(f32)
        post = rows_ref[b, 2 * EP :, :].astype(f32)
        for e in range(epis):
            at = slice(e * EP, (e + 1) * EP)
            s1 = spike(membrane1(b, e, post))
            s1_ref[j, at, :] = s1
            p2_ref[at, :] += fold(s1.astype(f32) * pre)

    def multiply(j):
        for copy in fetch(j):
            copy.wait()
        at = block_rows(j ^ me, width)
        s1 = s1_ref[j]
        acco_ref[...] += dot(s1, wo_ref[at, :])
        accs_ref[...] += dot(s1, ws_ref[at, :])

    rebuild(0)

    def body(j, _):
        multiply(j)
        rebuild(j + 1)
        return 0

    lax.fori_loop(0, tp - 1, body, 0)
    multiply(tp - 1)
    proj2 = sigma_scale * jnp.sum(p2_ref[...], axis=1, keepdims=True)
    for h, side_ref, acc_ref, s2_ref, mem_ref in (
        (0, so_ref, acco_ref, s2o_ref, memo_ref),
        (1, ss_ref, accs_ref, s2s_ref, mems_ref),
    ):
        leak = side_ref[lead : lead + 1, :]
        post = rows_ref[h ^ me, 2 * EP :, :].astype(f32)
        for e in range(epis):
            at = slice(e * EP, (e + 1) * EP)
            s1 = s1_ref[h, at, :]
            s1c_ref[h, at, :] = s1
            mem = leak * (membrane1(h ^ me, e, post) - s1.astype(f32)) + side_ref[2 * EP + e : 2 * EP + e + 1, :]
            mem = mem + acc_ref[at, :] + proj2[at, :] * post
            mem_ref[at, :] = mem
            s2_ref[at, :] = spike(mem)


def step2_call(me, base, got, w_rec, w_sib, proj1, side, side_sib, near, epis):
    tp, _, width = base.shape
    n = epis * EP
    return pl.pallas_call(
        functools.partial(step2_kernel, epis=epis),
        in_specs=[SM, VM, VM, HB, HB, VM, VM, VM, HB],
        out_specs=[VM] * 5,
        out_shape=[
            sds((n, width), bf16), sds((n, width), bf16), sds((n, width), f32), sds((n, width), f32),
            sds((2, n, width), bf16),
        ],
        scratch_shapes=[
            pltpu.VMEM((tp, n, width), bf16),
            pltpu.VMEM(w_sib.shape, bf16),
            pltpu.VMEM(w_sib.shape, bf16),
            pltpu.VMEM((n, width), f32),
            pltpu.VMEM((n, width), f32),
            pltpu.VMEM((n, 128), f32),
            pltpu.SemaphoreType.DMA((2, tp)),
        ],
        name="step2",
        **params(L_STEP2, 4 * n * tp * width * width, 4 * tp * width * width),
    )(me, base, got, w_rec, w_sib, proj1, side, side_sib, near)


def fetch_blocks(order, me, wo_hbm, ws_hbm, w_ref, sems):
    copies = []
    for n, v in enumerate(order):
        at = block_rows(v ^ me, wo_hbm.shape[1])
        for h, hbm in ((0, wo_hbm), (1, ws_hbm)):
            copies.append(pltpu.make_async_copy(hbm.at[at], w_ref.at[h, n], sems.at[h, n]))
    for copy in copies:
        copy.start()
    return copies


def add_blocks(order, me, blocks, copies, w_ref, rows_ref, acco_ref, accs_ref, p_ref):
    for n, v in enumerate(order):
        copies[2 * n].wait()
        copies[2 * n + 1].wait()
        block = blocks[n][...]
        acco_ref[...] += dot(block, w_ref[0, n])
        accs_ref[...] += dot(block, w_ref[1, n])
        pre = rows_ref[v ^ me, EP : 2 * EP, :].astype(f32)
        for r in range(0, block.shape[0], EP):
            p_ref[r : r + EP, :] += fold(block[r : r + EP, :].astype(f32) * pre)


def own_kernel(
    me_ref, s2o_ref, s2s_ref, wo_hbm, ws_hbm, rows_ref, s1c_ref, memo_ref, mems_ref, so_ref, ss_ref, pack_ref, near_ref,
    acco_ref, accs_ref, p_ref, read_ref, pair_ref, w_ref, sems, *, epis,
):
    blocks = (s2o_ref, s2s_ref)
    width = wo_hbm.shape[1]
    lead = so_ref.shape[0] - 8
    me = me_ref[0]
    copies = fetch_blocks([0, 1], me, wo_hbm, ws_hbm, w_ref, sems)
    pair_ref[0] = pack_ref[...]
    pair_ref[1] = near_ref[...]
    p_ref[...] = jnp.zeros_like(p_ref)
    sums = jnp.zeros((EP, 128), f32)
    for h, side_ref, mem_ref, acc_ref in ((0, so_ref, memo_ref, acco_ref), (1, ss_ref, mems_ref, accs_ref)):
        leak, read = side_ref[lead : lead + 1, :], side_ref[lead + 1 : lead + 2, :]
        s0 = rows_ref[h ^ me, :EP, :].astype(f32)
        total = jnp.broadcast_to(jnp.sum(s0, 0, keepdims=True), (EP, width))
        for e in range(epis):
            at = slice(e * EP, (e + 1) * EP)
            s2 = blocks[h][at, :].astype(f32)
            total += s1c_ref[h, at, :].astype(f32) + s2
            acc_ref[at, :] = leak * (mem_ref[at, :] - s2) + side_ref[3 * EP + e : 3 * EP + e + 1, :]
        sums += fold(total * read)
    read_ref[...] = sums
    add_blocks([0, 1], me, blocks, copies, w_ref, rows_ref, acco_ref, accs_ref, p_ref)


def own_call(me, s2o, s2s, w_rec, w_sib, rows, s1c, memo, mems, side, side_sib, pack, near, epis):
    n, width = s2o.shape
    return pl.pallas_call(
        functools.partial(own_kernel, epis=epis),
        in_specs=[SM, VM, VM, HB, HB] + [VM] * 8,
        out_specs=[VM] * 5,
        out_shape=[
            sds((n, width), f32), sds((n, width), f32), sds((n, 128), f32), sds((EP, 128), f32),
            sds((2,) + pack.shape, bf16),
        ],
        scratch_shapes=[pltpu.VMEM((2, 2, width, width), bf16), pltpu.SemaphoreType.DMA((2, 2))],
        name="own",
        **params(L_PART, 8 * n * width * width, 8 * width * width),
    )(me, s2o, s2s, w_rec, w_sib, rows, s1c, memo, mems, side, side_sib, pack, near)


def part_kernel(me_ref, *refs, order):
    blocks, refs = refs[: len(order)], refs[len(order) :]
    wo_hbm, ws_hbm, rows_ref, acco_in, accs_in, p_in, acco_ref, accs_ref, p_ref, w_ref, sems = refs
    me = me_ref[0]
    copies = fetch_blocks(order, me, wo_hbm, ws_hbm, w_ref, sems)
    acco_ref[...] = acco_in[...]
    accs_ref[...] = accs_in[...]
    p_ref[...] = p_in[...]
    add_blocks(order, me, blocks, copies, w_ref, rows_ref, acco_ref, accs_ref, p_ref)


def part_call(me, blocks, order, w_rec, w_sib, rows, acco, accs, proj):
    n, width = blocks[0].shape
    count = len(order)
    return pl.pallas_call(
        functools.partial(part_kernel, order=order),
        in_specs=[SM] + [VM] * count + [HB, HB] + [VM] * 4,
        out_specs=[VM] * 3,
        out_shape=[sds((n, width), f32), sds((n, width), f32), sds((n, 128), f32)],
        scratch_shapes=[pltpu.VMEM((2, count, width, width), bf16), pltpu.SemaphoreType.DMA((2, count))],
        name="part",
        **params(L_PART, 4 * n * count * width * width, 4 * count * width * width),
    )(me, *blocks, w_rec, w_sib, rows, acco, accs, proj)


def last_kernel(me_ref, *refs, order, epis, copies):
    blocks, refs = refs[: len(order)], refs[len(order) :]
    wo_hbm, ws_hbm, rows_ref, acco_in, accs_in, p_in, so_ref, ss_ref, read_ref, ranks_ref = refs[:10]
    note_ref, w_ref, acco_ref, accs_ref, p_ref, sems = refs[10:]
    lead = so_ref.shape[0] - 8
    me = me_ref[0]
    fetched = fetch_blocks(order, me, wo_hbm, ws_hbm, w_ref, sems)
    acco_ref[...] = acco_in[...]
    accs_ref[...] = accs_in[...]
    p_ref[...] = p_in[...]
    add_blocks(order, me, blocks, fetched, w_ref, rows_ref, acco_ref, accs_ref, p_ref)
    proj = sigma_scale * jnp.sum(p_ref[...], axis=1, keepdims=True)
    sums = read_ref[...]
    for h, side_ref, acc_ref in ((0, so_ref, acco_ref), (1, ss_ref, accs_ref)):
        read = side_ref[lead + 1 : lead + 2, :]
        post = rows_ref[h ^ me, 2 * EP :, :].astype(f32)
        total = jnp.zeros(post.shape, f32)
        for e in range(epis):
            at = slice(e * EP, (e + 1) * EP)
            total += spike(acc_ref[at, :] + proj[at, :] * post).astype(f32)
        sums += fold(total * read)
    sums = jnp.sum(sums, axis=1, keepdims=True)
    row = lax.broadcasted_iota(i32, (EP, 128), 0)
    lane = lax.broadcasted_iota(i32, (EP, 128), 1) & (EP - 1)
    flat = jnp.sum(jnp.where(row == lane, sums, 0.0), axis=0, keepdims=True)
    ranks = ranks_ref[...].astype(f32)
    wide = lax.broadcasted_iota(i32, (EP, 2 * EP), 1)
    chosen = wide == lax.broadcasted_iota(i32, (EP, 2 * EP), 0) + (me & 1) * EP
    mine = jnp.sum(jnp.where(chosen, ranks, 0.0), axis=1, keepdims=True)
    rank = jnp.sum(jnp.where(row == lane, mine, 0.0), axis=0, keepdims=True)
    odd = (lax.broadcasted_iota(i32, (2 * copies, 128), 0) & 1) == 1
    note_ref[...] = jnp.where(odd, rank, flat)


def last_call(me, blocks, order, w_rec, w_sib, rows, acco, accs, proj, side, side_sib, read, ranks, epis, copies):
    n, width = blocks[0].shape
    count = len(order)
    return pl.pallas_call(
        functools.partial(last_kernel, order=order, epis=epis, copies=copies),
        in_specs=[SM] + [VM] * count + [HB, HB] + [VM] * 8,
        out_specs=VM,
        out_shape=sds((2 * copies, 128), f32),
        scratch_shapes=[
            pltpu.VMEM((2, count, width, width), bf16),
            pltpu.VMEM((n, width), f32),
            pltpu.VMEM((n, width), f32),
            pltpu.VMEM((n, 128), f32),
            pltpu.SemaphoreType.DMA((2, count)),
        ],
        name="last",
        **params(L_LAST, 0, 0),
    )(me, *blocks, w_rec, w_sib, rows, acco, accs, proj, side, side_sib, read, ranks)


def tie_kernel(x_ref, after_ref, out_ref):
    pass


def tie_call(x, after):
    return pl.pallas_call(
        tie_kernel,
        in_specs=[HB, HB],
        out_specs=HB,
        out_shape=sds(x.shape, x.dtype),
        input_output_aliases={0: 0},
        name="tie",
        **params(8, 0, 1024),
    )(x, after)


def hand_kernel(x_ref, after_ref, out_ref):
    out_ref[...] = x_ref[...]


def hand_call(x, after):
    return pl.pallas_call(
        hand_kernel,
        in_specs=[VM, HB],
        out_specs=VM,
        out_shape=sds(x.shape, x.dtype),
        name="hand",
        **params(8, 0, 1024),
    )(x, after)


def prep_kernel(core_ref, *refs, pop):
    groups, (pret_ref, post_ref) = refs[:pop], refs[pop:]
    tp = groups[0].shape[1] - 2
    width = groups[0].shape[3]
    for b in range(tp):
        cols = jnp.concatenate([g[i, b] for g in groups for i in range(2)], 0)
        pret_ref[b * width : (b + 1) * width, :] = cols.astype(f32).T.astype(bf16)
    for d in range(2):
        for s in range(pop):
            at = (d * pop + s) * EP
            post_ref[at : at + EP, :] = groups[s // 2][s % 2, tp + (d ^ core_ref[0])]


def prep_call(core, groups, pop):
    _, blocks, _, width = groups[0].shape
    count = 2 * pop * EP
    return pl.pallas_call(
        functools.partial(prep_kernel, pop=pop),
        in_specs=[SM] + [VM] * len(groups),
        out_specs=[VM] * 2,
        out_shape=[sds(((blocks - 2) * width, count), bf16), sds((count, width), bf16)],
        name="prep",
        **params(16, count * blocks * width, 4 * count * blocks * width),
    )(core, *groups)


def grad_kernel(place_ref, note_ref, pret_ref, post_ref, grad_hbm, ret_ref, both_ref, grad_ref, sems, *, tp, pop, plays):
    count = post_ref.shape[0]
    plane, core = place_ref[0], place_ref[1]
    shift = tp.bit_length() - 1
    notes = note_ref[...]

    def where_from(shape):
        row = lax.broadcasted_iota(i32, shape, 0)
        return (row >> 1) >> shift, (row >> 1) & (tp - 1), row & 1, lax.broadcasted_iota(i32, shape, 1) >> 4

    wide = jnp.concatenate([notes] * (count // 128), 1) if count > 128 else notes
    place, unit, kind, group = where_from(wide.shape)
    match = (place == (plane ^ (group & (pop - 1)))) & ((unit & 1) == (core ^ (group >> (pop.bit_length() - 1))))
    total = jnp.sum(jnp.where(match & (kind == 0), wide, 0.0), 0, keepdims=True)
    rank = jnp.sum(jnp.where(match & (kind == 1) & (unit < 2), wide, 0.0), 0, keepdims=True)
    fitness = rank / (count - 1) - 0.5 + total / plays
    fitness = fitness * ((12.0 / count) ** 0.5)
    diag = lax.broadcasted_iota(i32, (count, count), 0) == lax.broadcasted_iota(i32, (count, count), 1)
    column = jnp.sum(jnp.where(diag, fitness, 0.0), 1, keepdims=True)
    weighted = post_ref[...].astype(f32) * column
    high = weighted.astype(bf16)
    both_ref[:count, :] = high
    both_ref[count:, :] = (weighted - high.astype(f32)).astype(bf16)

    inputs = pret_ref.shape[0]
    block = min(512, inputs)

    def out(i):
        at = block_rows(i, block)
        return pltpu.make_async_copy(grad_ref.at[at], grad_hbm.at[at], sems.at[i])

    def body(i, _):
        at = block_rows(i, block)
        pret = pret_ref[at, :]
        grad_ref[at, :] = dot(jnp.concatenate([pret, pret], 1), both_ref[...]).astype(bf16)
        out(i).start()
        return 0

    lax.fori_loop(0, inputs // block, body, 0)
    place, unit, kind, group = where_from(notes.shape)
    mine = (place == plane) & ((unit & 1) == group) & (kind == 0)
    ret_ref[...] = (jnp.sum(jnp.where(mine, notes, 0.0), 0, keepdims=True) / plays)[0, : ret_ref.shape[0]]
    lax.fori_loop(0, inputs // block, lambda i, _: (out(i).wait(), 0)[1], 0)


def grad_call(place, notes, pret, post, tp, pop, plays, members):
    inputs, count = pret.shape
    width = post.shape[1]
    return pl.pallas_call(
        functools.partial(grad_kernel, tp=tp, pop=pop, plays=plays),
        in_specs=[SM] + [VM] * 3,
        out_specs=[HB, VM],
        out_shape=[sds((inputs, width), bf16), sds((members,), f32)],
        scratch_shapes=[
            pltpu.VMEM((2 * count, width), bf16),
            pltpu.VMEM((inputs, width), bf16),
            pltpu.SemaphoreType.DMA((inputs // min(512, inputs),)),
        ],
        name="grad",
        **params(16, 4 * inputs * count * width, 2 * inputs * (count + width)),
    )(place, notes, pret, post)


def swap(x, axis, mask):
    return lax.ppermute(x, axis, [(i, i ^ mask) for i in range(lax.axis_size(axis))])


def shards(
    in_spikes, w_in, w_rec, leak_rate, neuron_bias, readout, pert_table, pert_idx, member_ranks
):
    steps, epis, inputs = in_spikes.shape
    members = pert_idx.shape[0]
    tp, pop = lax.axis_size("tp"), lax.axis_size("pop")
    assert steps == 4 and epis < EP and members == 2 * EP
    me, plane = lax.axis_index("tp"), lax.axis_index("pop")
    at = me[None].astype(i32)
    place = jnp.stack([plane, me & 1]).astype(i32)

    w_sib = swap(w_rec, "tp", 1)
    side, load, post_loc = drive_call(
        in_spikes, w_in, neuron_bias, leak_rate, readout, pert_table, pert_idx, tp
    )
    got = lax.all_to_all(load, "tp", 0, 0)
    w_sib = tie_call(w_sib, got)
    w_own = swap(w_sib, "tp", 1)
    side_sib = swap(side, "tp", 1)
    base = lax.all_to_all(base_call(got, w_rec, side), "tp", 0, 0)
    proj1, pack = proj_call(got, post_loc)
    near = swap(pack, "pop", 1)
    s2o, s2s, memo, mems, s1c = step2_call(at, base, got, w_own, w_sib, proj1, side, side_sib, near, epis)
    far, order = [], []
    if tp == 8:
        xa, yb = swap(s2o, "tp", 2), swap(s2s, "tp", 4)
        xb, ya = swap(s2s, "tp", 2), swap(s2o, "tp", 4)
    else:
        for mask in range(2, tp, 2):
            far += [swap(s2o, "tp", mask), swap(s2s, "tp", mask)]
            order += [mask, mask + 1]
    acco, accs, proj, read, pair = own_call(
        at, s2o, s2s, w_own, w_sib, got, s1c, memo, mems, side, side_sib, pack, near, epis
    )
    if tp == 8:
        xa, yb = tie_call(xa, pair), tie_call(yb, pair)
        far, order = [xa, yb], [2, 5]
        end, ends = [xb, ya, swap(xa, "tp", 4), swap(yb, "tp", 2)], [3, 4, 6, 7]
    else:
        far, end, order, ends = far[:-2], far[-2:], order[:-2], order[-2:]
    acco, accs, proj = part_call(at, far, order, w_own, w_sib, got, acco, accs, proj)
    notes = last_call(
        at, end, ends, w_own, w_sib, got, acco, accs, proj, side, side_sib, read, member_ranks[None], epis, pop * tp
    )
    groups, mask = [pair], 2
    while mask < pop:
        groups += [swap(g, "pop", mask) for g in groups]
        mask *= 2
    groups += [swap(g, "tp", 1) for g in groups[:1]] + [swap(hand_call(g, notes), "tp", 1) for g in groups[1:]]
    notes = lax.all_to_all(notes, ("pop", "tp"), 0, 0, tiled=True)
    pret, post_all = prep_call(place[1:], groups, pop)
    grad, returns = grad_call(place, notes, pret, post_all, tp, pop, epis * steps, members)
    return (returns, grad)


def solution(mesh):
    placed = (
        P(),
        P(None, "tp"),
        P(None, "tp"),
        P("tp"),
        P("tp"),
        P("tp"),
        P(None, "tp"),
        P("pop", None),
        P("pop"),
    )
    return jax.shard_map(
        shards, mesh=mesh, in_specs=placed, out_specs=(P("pop"), P(None, "tp")), check_vma=False
    )
```

```python
import functools

import jax
import jax.numpy as jnp
from jax import lax
from jax.experimental import pallas as pl
from jax.experimental.pallas import tpu as pltpu
from jax.sharding import PartitionSpec as P

sigma_scale = 0.01
f32 = jnp.float32
bf16 = jnp.bfloat16
i32 = jnp.int32
L_BASE = 48
L_STEP2 = 32
L_PART = 24
L_DRIVE = 58
L_LAST = 24
EP = 16


def spike(membrane):
    return (0.5 + 0.5 * jnp.tanh(2.0 * (membrane - 1.0))).astype(bf16)


def dot(a, b):
    return jnp.dot(a, b, preferred_element_type=f32)


def fold(x):
    parts = [x[:, i : i + 128] for i in range(0, x.shape[1], 128)]
    return functools.reduce(jnp.add, parts)


def params(mib, flops, nbytes):
    return dict(
        compiler_params=pltpu.CompilerParams(vmem_limit_bytes=mib * 2**20),
        cost_estimate=pl.CostEstimate(flops=flops, bytes_accessed=nbytes, transcendentals=0),
    )


VM = pl.BlockSpec(memory_space=pltpu.VMEM)
SM = pl.BlockSpec(memory_space=pltpu.SMEM)
HB = pl.BlockSpec(memory_space=pltpu.HBM)
sds = jax.ShapeDtypeStruct


def block_rows(b, width):
    return pl.ds(pl.multiple_of(b * width, width), width)


def drive_kernel(
    spk_hbm, win_hbm, bias_hbm, leak_hbm, read_hbm, table_hbm, idx_hbm,
    side_ref, load_ref, post_ref,
    spk, win, bias, leak, read, table, idx, acc_ref, sems,
):
    epis, steps, inputs = spk.shape
    tp = load_ref.shape[0]
    parts = 4
    depth = inputs // parts
    copies = []
    for k in range(parts):
        at = pl.ds(k * depth, depth)
        copies.append((spk_hbm.at[:, :, at], spk.at[:, :, at]))
        copies.append((win_hbm.at[at], win.at[at]))
    copies += [(table_hbm, table), (idx_hbm, idx), (bias_hbm, bias), (leak_hbm, leak), (read_hbm, read)]
    copies = [pltpu.make_async_copy(a, b, sems.at[n]) for n, (a, b) in enumerate(copies)]
    for copy in copies:
        copy.start()
    for k in range(parts):
        copies[2 * k].wait()
        copies[2 * k + 1].wait()
        at = slice(k * depth, (k + 1) * depth)
        x = spk[:, :, at].reshape(epis * steps, depth).astype(f32).astype(bf16)
        part = dot(x, win[at, :])
        total = part if k == 0 else total + part
    for copy in copies[2 * parts :]:
        copy.wait()
    total = total + bias[...]
    lanes = range(acc_ref.shape[0])
    for c in lanes:
        acc_ref[c] = total[:, c * 128 : (c + 1) * 128]
    blank = jnp.zeros((EP - epis, total.shape[1]), f32)
    for t in range(steps):
        drive = jnp.concatenate([acc_ref[c, pl.ds(t, epis, stride=steps), :] for c in lanes], 1)
        drive = jnp.concatenate([drive, blank], 0)
        side_ref[t * EP : (t + 1) * EP, :] = drive
        if t == 0:
            s0 = spike(drive).astype(f32)
            here = lax.broadcasted_iota(i32, s0.shape, 0) < epis
            s0 = jnp.where(here, s0, 0.0).astype(bf16)
            for j in range(tp):
                load_ref[j, :EP, :] = s0
    row = lax.broadcasted_iota(i32, (8, total.shape[1]), 0)
    side_ref[steps * EP :, :] = jnp.where(row == 0, leak[...], read[...])
    at = lax.broadcasted_iota(i32, (table.shape[0], idx.shape[1]), 0)
    pick = (((0,), (0,)), ((), ()))
    pre, post = (
        lax.dot_general(
            jnp.where(at == idx[n : n + 1, :], 1.0, 0.0).astype(bf16), table[...], pick, preferred_element_type=f32
        ).astype(bf16)
        for n in range(2)
    )
    for j in range(tp):
        own = slice((j % 2) * EP, (j % 2 + 1) * EP)
        load_ref[j, EP : 2 * EP, :] = pre[own]
        load_ref[j, 2 * EP :, :] = post[own]
    for c in range(2):
        post_ref[c] = post[c * EP : (c + 1) * EP]


def drive_call(in_spikes, w_in, bias, leak, read, table, idx, tp):
    steps, epis, inputs = in_spikes.shape
    width = w_in.shape[1]
    members = idx.shape[0]
    ins = [in_spikes.transpose(1, 0, 2), w_in, bias[None], leak[None], read[None], table, idx.T]
    return pl.pallas_call(
        drive_kernel,
        in_specs=[HB] * 7,
        out_specs=[VM] * 3,
        out_shape=[
            sds((steps * EP + 8, width), f32),
            sds((tp, 3 * EP, width), bf16),
            sds((2, EP, width), bf16),
        ],
        scratch_shapes=[pltpu.VMEM(x.shape, x.dtype) for x in ins]
        + [pltpu.VMEM((width // 128, steps * epis, 128), f32), pltpu.SemaphoreType.DMA((13,))],
        name="drive",
        **params(L_DRIVE, 2 * steps * EP * inputs * width, inputs * width * 2 + steps * EP * inputs * 4),
    )(*ins)


def base_kernel(got_ref, w_hbm, side_ref, out_ref, w_ref, sems):
    tp, _, width = got_ref.shape
    lead = side_ref.shape[0] - 8
    parts = 4
    depth = w_ref.shape[0] // parts
    copies = []
    for k in range(parts):
        at = pl.ds(k * depth, depth)
        copies.append(pltpu.make_async_copy(w_hbm.at[at], w_ref.at[at], sems.at[k]))
    for copy in copies:
        copy.start()
    mem0 = side_ref[0:EP, :]
    leak = side_ref[lead : lead + 1, :]
    base = leak * (mem0 - spike(mem0).astype(f32)) + side_ref[EP : 2 * EP, :]
    for k in range(parts):
        copies[k].wait()
        for j in range(k * tp // parts, (k + 1) * tp // parts):
            base += dot(got_ref[j, :EP, :], w_ref[j * width : (j + 1) * width, :])
    for i in range(tp):
        out_ref[i] = base


def base_call(got, w_rec, side):
    tp, _, width = got.shape
    return pl.pallas_call(
        base_kernel,
        in_specs=[VM, HB, VM],
        out_specs=VM,
        out_shape=sds((tp, EP, width), f32),
        scratch_shapes=[pltpu.VMEM(w_rec.shape, bf16), pltpu.SemaphoreType.DMA((4,))],
        name="base",
        **params(L_BASE, 2 * EP * tp * width * width, tp * width * width * 2),
    )(got, w_rec, side)


def proj_kernel(got_ref, post_ref, proj_ref, pack_ref):
    tp = got_ref.shape[0]
    proj = jnp.zeros((EP, EP), f32)
    for j in range(tp):
        pre = got_ref[j, EP : 2 * EP, :]
        proj += lax.dot_general(pre, got_ref[j, :EP, :], (((1,), (1,)), ((), ())), preferred_element_type=f32)
        pack_ref[j] = pre
    proj_ref[...] = sigma_scale * proj
    for c in range(2):
        pack_ref[tp + c] = post_ref[c]


def proj_call(got, post_loc):
    tp, _, width = got.shape
    return pl.pallas_call(
        proj_kernel,
        in_specs=[VM] * 2,
        out_specs=[VM] * 2,
        out_shape=[sds((EP, EP), f32), sds((tp + 2, EP, width), bf16)],
        name="proj",
        **params(8, 2 * EP * EP * tp * width, 4 * tp * EP * width),
    )(got, post_loc)


def step2_kernel(
    me_ref, base_ref, rows_ref, wo_hbm, ws_hbm, proj1_ref, so_ref, ss_ref, near_ref,
    s2o_ref, s2s_ref, memo_ref, mems_ref, s1c_ref,
    s1_ref, wo_ref, ws_ref, acco_ref, accs_ref, p2_ref, sems, *, epis,
):
    tp, _, width = base_ref.shape
    lead = so_ref.shape[0] - 8
    me = me_ref[0]

    def fetch(j):
        at = block_rows(j ^ me, width)
        return (
            pltpu.make_async_copy(wo_hbm.at[at], wo_ref.at[at], sems.at[0, j]),
            pltpu.make_async_copy(ws_hbm.at[at], ws_ref.at[at], sems.at[1, j]),
        )

    for j in range(tp):
        for copy in fetch(j):
            copy.start()

    def membrane1(b, e, post):
        return base_ref[b, e : e + 1, :] + proj1_ref[:, e : e + 1] * post

    p2_ref[...] = jnp.zeros_like(p2_ref)
    acco_ref[...] = jnp.zeros_like(acco_ref)
    accs_ref[...] = jnp.zeros_like(accs_ref)

    def rebuild(j):
        b = j ^ me
        pre = rows_ref[b, EP : 2 * EP, :].astype(f32)
        post = rows_ref[b, 2 * EP :, :].astype(f32)
        for e in range(epis):
            at = slice(e * EP, (e + 1) * EP)
            s1 = spike(membrane1(b, e, post))
            s1_ref[j, at, :] = s1
            p2_ref[at, :] += fold(s1.astype(f32) * pre)

    def multiply(j):
        for copy in fetch(j):
            copy.wait()
        at = block_rows(j ^ me, width)
        s1 = s1_ref[j]
        acco_ref[...] += dot(s1, wo_ref[at, :])
        accs_ref[...] += dot(s1, ws_ref[at, :])

    rebuild(0)

    def body(j, _):
        multiply(j)
        rebuild(j + 1)
        return 0

    lax.fori_loop(0, tp - 1, body, 0, unroll=True)
    multiply(tp - 1)
    proj2 = sigma_scale * jnp.sum(p2_ref[...], axis=1, keepdims=True)
    for h, side_ref, acc_ref, s2_ref, mem_ref in (
        (0, so_ref, acco_ref, s2o_ref, memo_ref),
        (1, ss_ref, accs_ref, s2s_ref, mems_ref),
    ):
        leak = side_ref[lead : lead + 1, :]
        post = rows_ref[h ^ me, 2 * EP :, :].astype(f32)
        for e in range(epis):
            at = slice(e * EP, (e + 1) * EP)
            s1 = s1_ref[h, at, :]
            s1c_ref[h, at, :] = s1
            mem = leak * (membrane1(h ^ me, e, post) - s1.astype(f32)) + side_ref[2 * EP + e : 2 * EP + e + 1, :]
            mem = mem + acc_ref[at, :] + proj2[at, :] * post
            mem_ref[at, :] = mem
            s2_ref[at, :] = spike(mem)


def step2_call(me, base, got, w_rec, w_sib, proj1, side, side_sib, near, epis):
    tp, _, width = base.shape
    n = epis * EP
    return pl.pallas_call(
        functools.partial(step2_kernel, epis=epis),
        in_specs=[SM, VM, VM, HB, HB, VM, VM, VM, HB],
        out_specs=[VM] * 5,
        out_shape=[
            sds((n, width), bf16), sds((n, width), bf16), sds((n, width), f32), sds((n, width), f32),
            sds((2, n, width), bf16),
        ],
        scratch_shapes=[
            pltpu.VMEM((tp, n, width), bf16),
            pltpu.VMEM(w_sib.shape, bf16),
            pltpu.VMEM(w_sib.shape, bf16),
            pltpu.VMEM((n, width), f32),
            pltpu.VMEM((n, width), f32),
            pltpu.VMEM((n, 128), f32),
            pltpu.SemaphoreType.DMA((2, tp)),
        ],
        name="step2",
        **params(L_STEP2, 4 * n * tp * width * width, 4 * tp * width * width),
    )(me, base, got, w_rec, w_sib, proj1, side, side_sib, near)


def fetch_blocks(order, me, wo_hbm, ws_hbm, w_ref, sems):
    copies = []
    for n, v in enumerate(order):
        at = block_rows(v ^ me, wo_hbm.shape[1])
        for h, hbm in ((0, wo_hbm), (1, ws_hbm)):
            copies.append(pltpu.make_async_copy(hbm.at[at], w_ref.at[h, n], sems.at[h, n]))
    for copy in copies:
        copy.start()
    return copies


def add_blocks(order, me, blocks, copies, w_ref, rows_ref, acco_ref, accs_ref, p_ref):
    for n, v in enumerate(order):
        for copy in copies[2 * n : 2 * n + 2]:
            copy.wait()
        block = blocks[n][...]
        acco_ref[...] += dot(block, w_ref[0, n])
        accs_ref[...] += dot(block, w_ref[1, n])
        pre = rows_ref[v ^ me, EP : 2 * EP, :].astype(f32)
        for r in range(0, block.shape[0], EP):
            p_ref[r : r + EP, :] += fold(block[r : r + EP, :].astype(f32) * pre)


def own_kernel(
    me_ref, s2o_ref, s2s_ref, wo_hbm, ws_hbm, rows_ref, s1c_ref, memo_ref, mems_ref, so_ref, ss_ref, pack_ref, near_ref,
    acco_ref, accs_ref, p_ref, read_ref, pair_ref, w_ref, sems, *, epis,
):
    blocks = (s2o_ref, s2s_ref)
    width = wo_hbm.shape[1]
    lead = so_ref.shape[0] - 8
    me = me_ref[0]
    copies = fetch_blocks([0, 1], me, wo_hbm, ws_hbm, w_ref, sems)
    pair_ref[0] = pack_ref[...]
    pair_ref[1] = near_ref[...]
    p_ref[...] = jnp.zeros_like(p_ref)
    sums = jnp.zeros((EP, 128), f32)
    for h, side_ref, mem_ref, acc_ref in ((0, so_ref, memo_ref, acco_ref), (1, ss_ref, mems_ref, accs_ref)):
        leak, read = side_ref[lead : lead + 1, :], side_ref[lead + 1 : lead + 2, :]
        s0 = rows_ref[h ^ me, :EP, :].astype(f32)
        total = jnp.broadcast_to(jnp.sum(s0, 0, keepdims=True), (EP, width))
        for e in range(epis):
            at = slice(e * EP, (e + 1) * EP)
            s2 = blocks[h][at, :].astype(f32)
            total += s1c_ref[h, at, :].astype(f32) + s2
            acc_ref[at, :] = leak * (mem_ref[at, :] - s2) + side_ref[3 * EP + e : 3 * EP + e + 1, :]
        sums += fold(total * read)
    read_ref[...] = sums
    add_blocks([0, 1], me, blocks, copies, w_ref, rows_ref, acco_ref, accs_ref, p_ref)


def own_call(me, s2o, s2s, w_rec, w_sib, rows, s1c, memo, mems, side, side_sib, pack, near, epis):
    n, width = s2o.shape
    return pl.pallas_call(
        functools.partial(own_kernel, epis=epis),
        in_specs=[SM, VM, VM, HB, HB] + [VM] * 8,
        out_specs=[VM] * 5,
        out_shape=[
            sds((n, width), f32), sds((n, width), f32), sds((n, 128), f32), sds((EP, 128), f32),
            sds((2,) + pack.shape, bf16),
        ],
        scratch_shapes=[pltpu.VMEM((2, 2, width, width), bf16), pltpu.SemaphoreType.DMA((2, 2))],
        name="own",
        **params(L_PART, 8 * n * width * width, 8 * width * width),
    )(me, s2o, s2s, w_rec, w_sib, rows, s1c, memo, mems, side, side_sib, pack, near)


def part_kernel(me_ref, *refs, order, tail):
    blocks, refs = refs[: len(order)], refs[len(order) :]
    wo_hbm, ws_hbm, rows_ref, acco_in, accs_in, p_in, acco_ref, accs_ref, p_ref, *rest = refs
    w_ref, sems = rest[-2:]
    me = me_ref[0]
    copies = fetch_blocks(order, me, wo_hbm, ws_hbm, w_ref, sems)
    if tail:
        later = fetch_blocks(tail, me, wo_hbm, ws_hbm, rest[0], rest[1])
    acco_ref[...] = acco_in[...]
    accs_ref[...] = accs_in[...]
    p_ref[...] = p_in[...]
    add_blocks(order, me, blocks, copies, w_ref, rows_ref, acco_ref, accs_ref, p_ref)
    if tail:
        for copy in later:
            copy.wait()


def part_call(me, blocks, order, w_rec, w_sib, rows, acco, accs, proj, tail=()):
    n, width = blocks[0].shape
    count = len(order)
    more = [sds((2, len(tail), width, width), bf16)] if tail else []
    sems = [pltpu.SemaphoreType.DMA((2, len(tail)))] if tail else []
    return pl.pallas_call(
        functools.partial(part_kernel, order=order, tail=tail),
        in_specs=[SM] + [VM] * count + [HB, HB] + [VM] * 4,
        out_specs=[VM] * (3 + len(more)),
        out_shape=[sds((n, width), f32), sds((n, width), f32), sds((n, 128), f32)] + more,
        scratch_shapes=sems + [pltpu.VMEM((2, count, width, width), bf16), pltpu.SemaphoreType.DMA((2, count))],
        name="part",
        **params(L_PART, 4 * n * count * width * width, 4 * count * width * width),
    )(me, *blocks, w_rec, w_sib, rows, acco, accs, proj)


def last_kernel(me_ref, *refs, order, epis, copies):
    blocks, refs = refs[: len(order)], refs[len(order) :]
    w_ref, rows_ref, acco_in, accs_in, p_in, so_ref, ss_ref, read_ref, ranks_ref = refs[:9]
    note_ref, acco_ref, accs_ref, p_ref = refs[9:]
    lead = so_ref.shape[0] - 8
    me = me_ref[0]
    acco_ref[...] = acco_in[...]
    accs_ref[...] = accs_in[...]
    p_ref[...] = p_in[...]
    add_blocks(order, me, blocks, [], w_ref, rows_ref, acco_ref, accs_ref, p_ref)
    proj = sigma_scale * jnp.sum(p_ref[...], axis=1, keepdims=True)
    sums = read_ref[...]
    for h, side_ref, acc_ref in ((0, so_ref, acco_ref), (1, ss_ref, accs_ref)):
        read = side_ref[lead + 1 : lead + 2, :]
        post = rows_ref[h ^ me, 2 * EP :, :].astype(f32)
        total = jnp.zeros(post.shape, f32)
        for e in range(epis):
            at = slice(e * EP, (e + 1) * EP)
            total += spike(acc_ref[at, :] + proj[at, :] * post).astype(f32)
        sums += fold(total * read)
    sums = jnp.sum(sums, axis=1, keepdims=True)
    row = lax.broadcasted_iota(i32, (EP, 128), 0)
    lane = lax.broadcasted_iota(i32, (EP, 128), 1) & (EP - 1)
    flat = jnp.sum(jnp.where(row == lane, sums, 0.0), axis=0, keepdims=True)
    ranks = ranks_ref[...].astype(f32)
    wide = lax.broadcasted_iota(i32, (EP, 2 * EP), 1)
    chosen = wide == lax.broadcasted_iota(i32, (EP, 2 * EP), 0) + (me & 1) * EP
    mine = jnp.sum(jnp.where(chosen, ranks, 0.0), axis=1, keepdims=True)
    rank = jnp.sum(jnp.where(row == lane, mine, 0.0), axis=0, keepdims=True)
    odd = (lax.broadcasted_iota(i32, (2 * copies, 128), 0) & 1) == 1
    note_ref[...] = jnp.where(odd, rank, flat)


def last_call(me, blocks, order, tail, rows, acco, accs, proj, side, side_sib, read, ranks, epis, copies):
    n, width = blocks[0].shape
    count = len(order)
    return pl.pallas_call(
        functools.partial(last_kernel, order=order, epis=epis, copies=copies),
        in_specs=[SM] + [VM] * (count + 9),
        out_specs=VM,
        out_shape=sds((2 * copies, 128), f32),
        scratch_shapes=[
            pltpu.VMEM((n, width), f32),
            pltpu.VMEM((n, width), f32),
            pltpu.VMEM((n, 128), f32),
        ],
        name="last",
        **params(L_LAST, 0, 0),
    )(me, *blocks, tail, rows, acco, accs, proj, side, side_sib, read, ranks)


def tie_kernel(x_ref, after_ref, out_ref):
    pass


def tie_call(x, after):
    return pl.pallas_call(
        tie_kernel,
        in_specs=[HB, HB],
        out_specs=HB,
        out_shape=sds(x.shape, x.dtype),
        input_output_aliases={0: 0},
        name="tie",
        **params(8, 0, 1024),
    )(x, after)


def hand_kernel(x_ref, after_ref, out_ref):
    out_ref[...] = x_ref[...]


def hand_call(x, after):
    return pl.pallas_call(
        hand_kernel,
        in_specs=[VM, HB],
        out_specs=VM,
        out_shape=sds(x.shape, x.dtype),
        name="hand",
        **params(8, 0, 1024),
    )(x, after)


def prep_kernel(core_ref, *refs, pop):
    groups, (pret_ref, post_ref) = refs[:pop], refs[pop:]
    tp = groups[0].shape[1] - 2
    width = groups[0].shape[3]
    for b in range(tp):
        cols = jnp.concatenate([g[i, b] for g in groups for i in range(2)], 0)
        pret_ref[b * width : (b + 1) * width, :] = cols.astype(f32).T.astype(bf16)
    for d in range(2):
        for s in range(pop):
            at = (d * pop + s) * EP
            post_ref[at : at + EP, :] = groups[s // 2][s % 2, tp + (d ^ core_ref[0])]


def prep_call(core, groups, pop):
    _, blocks, _, width = groups[0].shape
    count = 2 * pop * EP
    return pl.pallas_call(
        functools.partial(prep_kernel, pop=pop),
        in_specs=[SM] + [VM] * len(groups),
        out_specs=[VM] * 2,
        out_shape=[sds(((blocks - 2) * width, count), bf16), sds((count, width), bf16)],
        name="prep",
        **params(16, count * blocks * width, 4 * count * blocks * width),
    )(core, *groups)


def grad_kernel(place_ref, note_ref, pret_ref, post_ref, grad_hbm, ret_ref, both_ref, grad_ref, sems, *, tp, pop, plays):
    count = post_ref.shape[0]
    plane, core = place_ref[0], place_ref[1]
    shift = tp.bit_length() - 1
    notes = note_ref[...]

    def where_from(shape):
        row = lax.broadcasted_iota(i32, shape, 0)
        return (row >> 1) >> shift, (row >> 1) & (tp - 1), row & 1, lax.broadcasted_iota(i32, shape, 1) >> 4

    wide = jnp.concatenate([notes] * (count // 128), 1) if count > 128 else notes
    place, unit, kind, group = where_from(wide.shape)
    match = (place == (plane ^ (group & (pop - 1)))) & ((unit & 1) == (core ^ (group >> (pop.bit_length() - 1))))
    total = jnp.sum(jnp.where(match & (kind == 0), wide, 0.0), 0, keepdims=True)
    rank = jnp.sum(jnp.where(match & (kind == 1) & (unit < 2), wide, 0.0), 0, keepdims=True)
    fitness = rank / (count - 1) - 0.5 + total / plays
    fitness = fitness * ((12.0 / count) ** 0.5)
    diag = lax.broadcasted_iota(i32, (count, count), 0) == lax.broadcasted_iota(i32, (count, count), 1)
    column = jnp.sum(jnp.where(diag, fitness, 0.0), 1, keepdims=True)
    weighted = post_ref[...].astype(f32) * column
    high = weighted.astype(bf16)
    both_ref[:count, :] = high
    both_ref[count:, :] = (weighted - high.astype(f32)).astype(bf16)

    inputs = pret_ref.shape[0]
    block = min(512, inputs)

    def out(i):
        at = block_rows(i, block)
        return pltpu.make_async_copy(grad_ref.at[at], grad_hbm.at[at], sems.at[i])

    def body(i, _):
        at = block_rows(i, block)
        pret = pret_ref[at, :]
        grad_ref[at, :] = dot(jnp.concatenate([pret, pret], 1), both_ref[...]).astype(bf16)
        out(i).start()
        return 0

    lax.fori_loop(0, inputs // block, body, 0, unroll=True)
    place, unit, kind, group = where_from(notes.shape)
    mine = (place == plane) & ((unit & 1) == group) & (kind == 0)
    ret_ref[...] = (jnp.sum(jnp.where(mine, notes, 0.0), 0, keepdims=True) / plays)[0, : ret_ref.shape[0]]
    lax.fori_loop(0, inputs // block, lambda i, _: (out(i).wait(), 0)[1], 0)


def grad_call(place, notes, pret, post, tp, pop, plays, members):
    inputs, count = pret.shape
    width = post.shape[1]
    return pl.pallas_call(
        functools.partial(grad_kernel, tp=tp, pop=pop, plays=plays),
        in_specs=[SM] + [VM] * 3,
        out_specs=[HB, VM],
        out_shape=[sds((inputs, width), bf16), sds((members,), f32)],
        scratch_shapes=[
            pltpu.VMEM((2 * count, width), bf16),
            pltpu.VMEM((inputs, width), bf16),
            pltpu.SemaphoreType.DMA((inputs // min(512, inputs),)),
        ],
        name="grad",
        **params(16, 4 * inputs * count * width, 2 * inputs * (count + width)),
    )(place, notes, pret, post)


def swap(x, axis, mask):
    return lax.ppermute(x, axis, [(i, i ^ mask) for i in range(lax.axis_size(axis))])


def shards(
    in_spikes, w_in, w_rec, leak_rate, neuron_bias, readout, pert_table, pert_idx, member_ranks
):
    steps, epis, inputs = in_spikes.shape
    members = pert_idx.shape[0]
    tp, pop = lax.axis_size("tp"), lax.axis_size("pop")
    assert steps == 4 and epis < EP and members == 2 * EP
    me, plane = lax.axis_index("tp"), lax.axis_index("pop")
    at = me[None].astype(i32)
    place = jnp.stack([plane, me & 1]).astype(i32)

    w_sib = swap(w_rec, "tp", 1)
    side, load, post_loc = drive_call(
        in_spikes, w_in, neuron_bias, leak_rate, readout, pert_table, pert_idx, tp
    )
    got = lax.all_to_all(load, "tp", 0, 0)
    w_sib = tie_call(w_sib, got)
    w_own = swap(w_sib, "tp", 1)
    side_sib = swap(side, "tp", 1)
    base = lax.all_to_all(base_call(got, w_rec, side), "tp", 0, 0)
    proj1, pack = proj_call(got, post_loc)
    near = swap(pack, "pop", 1)
    s2o, s2s, memo, mems, s1c = step2_call(at, base, got, w_own, w_sib, proj1, side, side_sib, near, epis)
    far, order = [], []
    if tp == 8:
        xa, yb = swap(s2o, "tp", 2), swap(s2s, "tp", 4)
        xb, ya = swap(s2s, "tp", 2), swap(s2o, "tp", 4)
    else:
        for mask in range(2, tp, 2):
            far += [swap(s2o, "tp", mask), swap(s2s, "tp", mask)]
            order += [mask, mask + 1]
    acco, accs, proj, read, pair = own_call(
        at, s2o, s2s, w_own, w_sib, got, s1c, memo, mems, side, side_sib, pack, near, epis
    )
    if tp == 8:
        xa, yb = tie_call(xa, pair), tie_call(yb, pair)
        far, order = [xa, yb], [2, 5]
        end, ends = [swap(xa, "tp", 4), swap(yb, "tp", 2)], [6, 7]
    else:
        far, end, order, ends = far[:-2], far[-2:], order[:-2], order[-2:]
    acco, accs, proj, tail = part_call(at, far, order, w_own, w_sib, got, acco, accs, proj, tuple(ends))
    if tp == 8:
        acco, accs, proj = part_call(at, [xb, ya], [3, 4], w_own, w_sib, got, acco, accs, proj)
    notes = last_call(
        at, end, ends, tail, got, acco, accs, proj, side, side_sib, read, member_ranks[None], epis, pop * tp
    )
    groups, mask = [pair], 2
    while mask < pop:
        groups += [swap(g, "pop", mask) for g in groups]
        mask *= 2
    groups += [swap(g, "tp", 1) for g in groups[:1]] + [swap(hand_call(g, notes), "tp", 1) for g in groups[1:]]
    notes = lax.all_to_all(notes, ("pop", "tp"), 0, 0, tiled=True)
    pret, post_all = prep_call(place[1:], groups, pop)
    grad, returns = grad_call(place, notes, pret, post_all, tp, pop, epis * steps, members)
    return (returns, grad)


def solution(mesh):
    placed = (
        P(),
        P(None, "tp"),
        P(None, "tp"),
        P("tp"),
        P("tp"),
        P("tp"),
        P(None, "tp"),
        P("pop", None),
        P("pop"),
    )
    return jax.shard_map(
        shards, mesh=mesh, in_specs=placed, out_specs=(P("pop"), P(None, "tp")), check_vma=False
    )
```

```python
import functools

import jax
import jax.numpy as jnp
from jax import lax
from jax.experimental import pallas as pl
from jax.experimental.pallas import tpu as pltpu
from jax.sharding import PartitionSpec as P

sigma_scale = 0.01
f32 = jnp.float32
bf16 = jnp.bfloat16
i32 = jnp.int32
L_BASE = 58
L_STEP2 = 32
L_PART = 24
L_DRIVE = 58
L_LAST = 24
EP = 16


def spike(membrane):
    return (0.5 + 0.5 * jnp.tanh(2.0 * (membrane - 1.0))).astype(bf16)


def dot(a, b):
    return jnp.dot(a, b, preferred_element_type=f32)


def fold(x):
    parts = [x[:, i : i + 128] for i in range(0, x.shape[1], 128)]
    return functools.reduce(jnp.add, parts)


def params(mib, flops, nbytes):
    return dict(
        compiler_params=pltpu.CompilerParams(vmem_limit_bytes=mib * 2**20),
        cost_estimate=pl.CostEstimate(flops=flops, bytes_accessed=nbytes, transcendentals=0),
    )


VM = pl.BlockSpec(memory_space=pltpu.VMEM)
HB = pl.BlockSpec(memory_space=pltpu.HBM)
sds = jax.ShapeDtypeStruct


def block_rows(b, width):
    return pl.ds(pl.multiple_of(b * width, width), width)


def drive_kernel(
    spk_hbm, win_hbm, bias_hbm, leak_hbm, read_hbm, table_hbm, idx_hbm,
    side_ref, load_ref, post_ref,
    spk, win, bias, leak, read, table, idx, acc_ref, sems,
):
    epis, steps, inputs = spk.shape
    tp = load_ref.shape[0]
    parts = 8
    depth = inputs // parts
    copies = []
    for k in range(parts):
        at = pl.ds(k * depth, depth)
        copies.append((spk_hbm.at[:, :, at], spk.at[:, :, at]))
        copies.append((win_hbm.at[at], win.at[at]))
    copies += [(table_hbm, table), (idx_hbm, idx), (bias_hbm, bias), (leak_hbm, leak), (read_hbm, read)]
    copies = [pltpu.make_async_copy(a, b, sems.at[n]) for n, (a, b) in enumerate(copies)]
    for copy in copies:
        copy.start()
    for k in range(parts):
        copies[2 * k].wait()
        copies[2 * k + 1].wait()
        at = slice(k * depth, (k + 1) * depth)
        x = spk[:, :, at].reshape(epis * steps, depth).astype(f32).astype(bf16)
        part = dot(x, win[at, :])
        total = part if k == 0 else total + part
    for copy in copies[2 * parts :]:
        copy.wait()
    total = total + bias[...]
    lanes = range(acc_ref.shape[0])
    for c in lanes:
        acc_ref[c] = total[:, c * 128 : (c + 1) * 128]
    blank = jnp.zeros((EP - epis, total.shape[1]), f32)
    for t in range(steps):
        drive = jnp.concatenate([acc_ref[c, pl.ds(t, epis, stride=steps), :] for c in lanes], 1)
        drive = jnp.concatenate([drive, blank], 0)
        side_ref[t * EP : (t + 1) * EP, :] = drive
        if t == 0:
            s0 = spike(drive).astype(f32)
            here = lax.broadcasted_iota(i32, s0.shape, 0) < epis
            s0 = jnp.where(here, s0, 0.0).astype(bf16)
            for j in range(tp):
                load_ref[j, :EP, :] = s0
    row = lax.broadcasted_iota(i32, (8, total.shape[1]), 0)
    side_ref[steps * EP :, :] = jnp.where(row == 0, leak[...], read[...])
    at = lax.broadcasted_iota(i32, (table.shape[0], idx.shape[1]), 0)
    pick = (((0,), (0,)), ((), ()))
    pre, post = (
        lax.dot_general(
            jnp.where(at == idx[n : n + 1, :], 1.0, 0.0).astype(bf16), table[...], pick, preferred_element_type=f32
        ).astype(bf16)
        for n in range(2)
    )
    for j in range(tp):
        own = slice((j % 2) * EP, (j % 2 + 1) * EP)
        load_ref[j, EP : 2 * EP, :] = pre[own]
        load_ref[j, 2 * EP :, :] = post[own]
    for c in range(2):
        post_ref[c] = post[c * EP : (c + 1) * EP]


def drive_call(in_spikes, w_in, bias, leak, read, table, idx, tp):
    steps, epis, inputs = in_spikes.shape
    width = w_in.shape[1]
    members = idx.shape[0]
    ins = [in_spikes.transpose(1, 0, 2), w_in, bias[None], leak[None], read[None], table, idx.T]
    return pl.pallas_call(
        drive_kernel,
        in_specs=[HB] * 7,
        out_specs=[VM] * 3,
        out_shape=[
            sds((steps * EP + 8, width), f32),
            sds((tp, 3 * EP, width), bf16),
            sds((2, EP, width), bf16),
        ],
        scratch_shapes=[pltpu.VMEM(x.shape, x.dtype) for x in ins]
        + [pltpu.VMEM((width // 128, steps * epis, 128), f32), pltpu.SemaphoreType.DMA((21,))],
        name="drive",
        **params(L_DRIVE, 2 * steps * EP * inputs * width, inputs * width * 2 + steps * EP * inputs * 4),
    )(*ins)


def base_kernel(got_hbm, w_hbm, side_hbm, out_ref, got_ref, w_ref, side_ref, sems):
    tp, _, width = got_ref.shape
    lead = side_ref.shape[0] - 8
    copies = [(got_hbm.at[:, pl.ds(0, EP)], got_ref)]
    for j in range(tp):
        at = pl.ds(j * width, width)
        copies.append((w_hbm.at[at], w_ref.at[at]))
    copies.append((side_hbm, side_ref))
    copies = [pltpu.make_async_copy(a, b, sems.at[n]) for n, (a, b) in enumerate(copies)]
    for copy in copies:
        copy.start()
    copies[0].wait()
    base = jnp.zeros((EP, width), f32)
    for j in range(tp):
        copies[j + 1].wait()
        base += dot(got_ref[j], w_ref[j * width : (j + 1) * width, :])
    copies[-1].wait()
    mem0 = side_ref[0:EP, :]
    leak = side_ref[lead : lead + 1, :]
    base += leak * (mem0 - spike(mem0).astype(f32)) + side_ref[EP : 2 * EP, :]
    for i in range(tp):
        out_ref[i] = base


def base_call(got, w_rec, side):
    tp, _, width = got.shape
    return pl.pallas_call(
        base_kernel,
        in_specs=[HB, HB, HB],
        out_specs=VM,
        out_shape=sds((tp, EP, width), f32),
        scratch_shapes=[
            pltpu.VMEM((tp, EP, width), bf16),
            pltpu.VMEM(w_rec.shape, bf16),
            pltpu.VMEM(side.shape, f32),
            pltpu.SemaphoreType.DMA((tp + 2,)),
        ],
        name="base",
        **params(L_BASE, 2 * EP * tp * width * width, tp * width * width * 2),
    )(got, w_rec, side)


def proj_kernel(got_ref, post_ref, proj_ref, pack_ref):
    tp = got_ref.shape[0]
    proj = jnp.zeros((EP, EP), f32)
    for j in range(tp):
        pre = got_ref[j, EP : 2 * EP, :]
        proj += lax.dot_general(pre, got_ref[j, :EP, :], (((1,), (1,)), ((), ())), preferred_element_type=f32)
        pack_ref[j] = pre
    proj_ref[...] = sigma_scale * proj
    for c in range(2):
        pack_ref[tp + c] = post_ref[c]


def proj_call(got, post_loc):
    tp, _, width = got.shape
    return pl.pallas_call(
        proj_kernel,
        in_specs=[VM] * 2,
        out_specs=[VM] * 2,
        out_shape=[sds((EP, EP), f32), sds((tp + 2, EP, width), bf16)],
        name="proj",
        **params(8, 2 * EP * EP * tp * width, 4 * tp * EP * width),
    )(got, post_loc)


def step2_kernel(
    base_ref, rows_ref, wo_hbm, ws_hbm, proj1_ref, so_ref, ss_ref,
    s2o_ref, s2s_ref, memo_ref, mems_ref, s1c_ref,
    s1_ref, wo_ref, ws_ref, acco_ref, accs_ref, p2_ref, sems, *, epis,
):
    tp, _, width = base_ref.shape
    lead = so_ref.shape[0] - 8
    me = lax.axis_index("tp")

    def fetch(j):
        at = block_rows(j ^ me, width)
        return (
            pltpu.make_async_copy(wo_hbm.at[at], wo_ref.at[at], sems.at[0, j]),
            pltpu.make_async_copy(ws_hbm.at[at], ws_ref.at[at], sems.at[1, j]),
        )

    for j in range(tp):
        for copy in fetch(j):
            copy.start()

    def membrane1(b, e, post):
        return base_ref[b, e : e + 1, :] + proj1_ref[:, e : e + 1] * post

    p2_ref[...] = jnp.zeros_like(p2_ref)
    acco_ref[...] = jnp.zeros_like(acco_ref)
    accs_ref[...] = jnp.zeros_like(accs_ref)

    def rebuild(j):
        b = j ^ me
        pre = rows_ref[b, EP : 2 * EP, :].astype(f32)
        post = rows_ref[b, 2 * EP :, :].astype(f32)
        for e in range(epis):
            at = slice(e * EP, (e + 1) * EP)
            s1 = spike(membrane1(b, e, post))
            s1_ref[j, at, :] = s1
            p2_ref[at, :] += fold(s1.astype(f32) * pre)

    def multiply(j):
        for copy in fetch(j):
            copy.wait()
        at = block_rows(j ^ me, width)
        s1 = s1_ref[j]
        acco_ref[...] += dot(s1, wo_ref[at, :])
        accs_ref[...] += dot(s1, ws_ref[at, :])

    rebuild(0)

    def body(j, _):
        multiply(j)
        rebuild(j + 1)
        return 0

    lax.fori_loop(0, tp - 1, body, 0, unroll=True)
    multiply(tp - 1)
    proj2 = sigma_scale * jnp.sum(p2_ref[...], axis=1, keepdims=True)
    for h, side_ref, acc_ref, s2_ref, mem_ref in (
        (0, so_ref, acco_ref, s2o_ref, memo_ref),
        (1, ss_ref, accs_ref, s2s_ref, mems_ref),
    ):
        leak = side_ref[lead : lead + 1, :]
        post = rows_ref[h ^ me, 2 * EP :, :].astype(f32)
        for e in range(epis):
            at = slice(e * EP, (e + 1) * EP)
            s1 = s1_ref[h, at, :]
            s1c_ref[h, at, :] = s1
            mem = leak * (membrane1(h ^ me, e, post) - s1.astype(f32)) + side_ref[2 * EP + e : 2 * EP + e + 1, :]
            mem = mem + acc_ref[at, :] + proj2[at, :] * post
            mem_ref[at, :] = mem
            s2_ref[at, :] = spike(mem)


def step2_call(base, got, w_rec, w_sib, proj1, side, side_sib, epis):
    tp, _, width = base.shape
    n = epis * EP
    return pl.pallas_call(
        functools.partial(step2_kernel, epis=epis),
        in_specs=[VM, VM, HB, HB, VM, VM, VM],
        out_specs=[VM] * 5,
        out_shape=[
            sds((n, width), bf16), sds((n, width), bf16), sds((n, width), f32), sds((n, width), f32),
            sds((2, n, width), bf16),
        ],
        scratch_shapes=[
            pltpu.VMEM((tp, n, width), bf16),
            pltpu.VMEM(w_sib.shape, bf16),
            pltpu.VMEM(w_sib.shape, bf16),
            pltpu.VMEM((n, width), f32),
            pltpu.VMEM((n, width), f32),
            pltpu.VMEM((n, 128), f32),
            pltpu.SemaphoreType.DMA((2, tp)),
        ],
        name="step2",
        **params(L_STEP2, 4 * n * tp * width * width, 4 * tp * width * width),
    )(base, got, w_rec, w_sib, proj1, side, side_sib)


def fetch_blocks(order, me, wo_hbm, ws_hbm, w_ref, sems):
    copies = []
    for n, v in enumerate(order):
        at = block_rows(v ^ me, wo_hbm.shape[1])
        for h, hbm in ((0, wo_hbm), (1, ws_hbm)):
            copies.append(pltpu.make_async_copy(hbm.at[at], w_ref.at[h, n], sems.at[h, n]))
    for copy in copies:
        copy.start()
    return copies


def add_blocks(order, me, blocks, copies, w_ref, rows_ref, acco_ref, accs_ref, p_ref):
    for n, v in enumerate(order):
        for copy in copies[2 * n : 2 * n + 2]:
            copy.wait()
        block = blocks[n][...]
        acco_ref[...] += dot(block, w_ref[0, n])
        accs_ref[...] += dot(block, w_ref[1, n])
        pre = rows_ref[v ^ me, EP : 2 * EP, :].astype(f32)
        for r in range(0, block.shape[0], EP):
            p_ref[r : r + EP, :] += fold(block[r : r + EP, :].astype(f32) * pre)


def own_kernel(
    s2o_ref, s2s_ref, wo_hbm, ws_hbm, rows_ref, s1c_ref, memo_ref, mems_ref, so_ref, ss_ref, pack_ref, near_ref,
    acco_ref, accs_ref, p_ref, read_ref, pair_ref, w_ref, sems, *, epis,
):
    blocks = (s2o_ref, s2s_ref)
    width = wo_hbm.shape[1]
    lead = so_ref.shape[0] - 8
    me = lax.axis_index("tp")
    copies = fetch_blocks([0, 1], me, wo_hbm, ws_hbm, w_ref, sems)
    pair_ref[0] = pack_ref[...]
    pair_ref[1] = near_ref[...]
    p_ref[...] = jnp.zeros_like(p_ref)
    sums = jnp.zeros((EP, 128), f32)
    for h, side_ref, mem_ref, acc_ref in ((0, so_ref, memo_ref, acco_ref), (1, ss_ref, mems_ref, accs_ref)):
        leak, read = side_ref[lead : lead + 1, :], side_ref[lead + 1 : lead + 2, :]
        s0 = rows_ref[h ^ me, :EP, :].astype(f32)
        total = jnp.broadcast_to(jnp.sum(s0, 0, keepdims=True), (EP, width))
        for e in range(epis):
            at = slice(e * EP, (e + 1) * EP)
            s2 = blocks[h][at, :].astype(f32)
            total += s1c_ref[h, at, :].astype(f32) + s2
            acc_ref[at, :] = leak * (mem_ref[at, :] - s2) + side_ref[3 * EP + e : 3 * EP + e + 1, :]
        sums += fold(total * read)
    read_ref[...] = sums
    add_blocks([0, 1], me, blocks, copies, w_ref, rows_ref, acco_ref, accs_ref, p_ref)


def own_call(s2o, s2s, w_rec, w_sib, rows, s1c, memo, mems, side, side_sib, pack, near, epis):
    n, width = s2o.shape
    return pl.pallas_call(
        functools.partial(own_kernel, epis=epis),
        in_specs=[VM, VM, HB, HB] + [VM] * 8,
        out_specs=[VM] * 5,
        out_shape=[
            sds((n, width), f32), sds((n, width), f32), sds((n, 128), f32), sds((EP, 128), f32),
            sds((2,) + pack.shape, bf16),
        ],
        scratch_shapes=[pltpu.VMEM((2, 2, width, width), bf16), pltpu.SemaphoreType.DMA((2, 2))],
        name="own",
        **params(L_PART, 8 * n * width * width, 8 * width * width),
    )(s2o, s2s, w_rec, w_sib, rows, s1c, memo, mems, side, side_sib, pack, near)


def part_kernel(*refs, order, tail):
    blocks, refs = refs[: len(order)], refs[len(order) :]
    wo_hbm, ws_hbm, rows_ref, acco_in, accs_in, p_in, acco_ref, accs_ref, p_ref, *rest = refs
    w_ref, sems = rest[-2:]
    me = lax.axis_index("tp")
    copies = fetch_blocks(order, me, wo_hbm, ws_hbm, w_ref, sems)
    if tail:
        later = fetch_blocks(tail, me, wo_hbm, ws_hbm, rest[0], rest[1])
    acco_ref[...] = acco_in[...]
    accs_ref[...] = accs_in[...]
    p_ref[...] = p_in[...]
    add_blocks(order, me, blocks, copies, w_ref, rows_ref, acco_ref, accs_ref, p_ref)
    if tail:
        for copy in later:
            copy.wait()


def part_call(blocks, order, w_rec, w_sib, rows, acco, accs, proj, tail=()):
    n, width = blocks[0].shape
    count = len(order)
    more = [sds((2, len(tail), width, width), bf16)] if tail else []
    sems = [pltpu.SemaphoreType.DMA((2, len(tail)))] if tail else []
    return pl.pallas_call(
        functools.partial(part_kernel, order=order, tail=tail),
        in_specs=[VM] * count + [HB, HB] + [VM] * 4,
        out_specs=[VM] * (3 + len(more)),
        out_shape=[sds((n, width), f32), sds((n, width), f32), sds((n, 128), f32)] + more,
        scratch_shapes=sems + [pltpu.VMEM((2, count, width, width), bf16), pltpu.SemaphoreType.DMA((2, count))],
        name="part",
        **params(L_PART, 4 * n * count * width * width, 4 * count * width * width),
    )(*blocks, w_rec, w_sib, rows, acco, accs, proj)


def last_kernel(*refs, order, epis, copies):
    blocks, refs = refs[: len(order)], refs[len(order) :]
    w_ref, rows_ref, acco_in, accs_in, p_in, so_ref, ss_ref, read_ref, ranks_ref = refs[:9]
    note_ref, acco_ref, accs_ref, p_ref = refs[9:]
    lead = so_ref.shape[0] - 8
    me = lax.axis_index("tp")
    acco_ref[...] = acco_in[...]
    accs_ref[...] = accs_in[...]
    p_ref[...] = p_in[...]
    add_blocks(order, me, blocks, [], w_ref, rows_ref, acco_ref, accs_ref, p_ref)
    proj = sigma_scale * jnp.sum(p_ref[...], axis=1, keepdims=True)
    sums = read_ref[...]
    for h, side_ref, acc_ref in ((0, so_ref, acco_ref), (1, ss_ref, accs_ref)):
        read = side_ref[lead + 1 : lead + 2, :]
        post = rows_ref[h ^ me, 2 * EP :, :].astype(f32)
        total = jnp.zeros(post.shape, f32)
        for e in range(epis):
            at = slice(e * EP, (e + 1) * EP)
            total += spike(acc_ref[at, :] + proj[at, :] * post).astype(f32)
        sums += fold(total * read)
    sums = jnp.sum(sums, axis=1, keepdims=True)
    row = lax.broadcasted_iota(i32, (EP, 128), 0)
    lane = lax.broadcasted_iota(i32, (EP, 128), 1) & (EP - 1)
    flat = jnp.sum(jnp.where(row == lane, sums, 0.0), axis=0, keepdims=True)
    ranks = ranks_ref[...].astype(f32)
    wide = lax.broadcasted_iota(i32, (EP, 2 * EP), 1)
    chosen = wide == lax.broadcasted_iota(i32, (EP, 2 * EP), 0) + (me & 1) * EP
    mine = jnp.sum(jnp.where(chosen, ranks, 0.0), axis=1, keepdims=True)
    rank = jnp.sum(jnp.where(row == lane, mine, 0.0), axis=0, keepdims=True)
    odd = (lax.broadcasted_iota(i32, (2 * copies, 128), 0) & 1) == 1
    note_ref[...] = jnp.where(odd, rank, flat)


def last_call(blocks, order, tail, rows, acco, accs, proj, side, side_sib, read, ranks, epis, copies):
    n, width = blocks[0].shape
    count = len(order)
    return pl.pallas_call(
        functools.partial(last_kernel, order=order, epis=epis, copies=copies),
        in_specs=[VM] * (count + 9),
        out_specs=VM,
        out_shape=sds((2 * copies, 128), f32),
        scratch_shapes=[
            pltpu.VMEM((n, width), f32),
            pltpu.VMEM((n, width), f32),
            pltpu.VMEM((n, 128), f32),
        ],
        name="last",
        **params(L_LAST, 0, 0),
    )(*blocks, tail, rows, acco, accs, proj, side, side_sib, read, ranks)


def tie_kernel(x_ref, after_ref, out_ref):
    pass


def tie_call(x, after):
    return pl.pallas_call(
        tie_kernel,
        in_specs=[HB, HB],
        out_specs=HB,
        out_shape=sds(x.shape, x.dtype),
        input_output_aliases={0: 0},
        name="tie",
        **params(8, 0, 1024),
    )(x, after)


def hand_kernel(x_ref, after_ref, out_ref):
    out_ref[...] = x_ref[...]


def hand_call(x, after):
    return pl.pallas_call(
        hand_kernel,
        in_specs=[VM, HB],
        out_specs=VM,
        out_shape=sds(x.shape, x.dtype),
        name="hand",
        **params(8, 0, 1024),
    )(x, after)


def prep_kernel(*refs, pop):
    groups, (pret_ref, post_ref) = refs[:pop], refs[pop:]
    tp = groups[0].shape[1] - 2
    width = groups[0].shape[3]
    for b in range(tp):
        cols = jnp.concatenate([g[i, b] for g in groups for i in range(2)], 0)
        pret_ref[b * width : (b + 1) * width, :] = cols.astype(f32).T.astype(bf16)
    for d in range(2):
        for s in range(pop):
            at = (d * pop + s) * EP
            post_ref[at : at + EP, :] = groups[s // 2][s % 2, tp + (d ^ (lax.axis_index("tp") & 1))]


def prep_call(groups, pop):
    _, blocks, _, width = groups[0].shape
    count = 2 * pop * EP
    return pl.pallas_call(
        functools.partial(prep_kernel, pop=pop),
        in_specs=[VM] * len(groups),
        out_specs=[VM] * 2,
        out_shape=[sds(((blocks - 2) * width, count), bf16), sds((count, width), bf16)],
        name="prep",
        **params(16, count * blocks * width, 4 * count * blocks * width),
    )(*groups)


def grad_kernel(note_ref, pret_ref, post_ref, grad_hbm, ret_ref, both_ref, grad_ref, sems, *, tp, pop, plays):
    count = post_ref.shape[0]
    plane, core = lax.axis_index("pop"), lax.axis_index("tp") & 1
    shift = tp.bit_length() - 1
    notes = note_ref[...]

    def where_from(shape):
        row = lax.broadcasted_iota(i32, shape, 0)
        return (row >> 1) >> shift, (row >> 1) & (tp - 1), row & 1, lax.broadcasted_iota(i32, shape, 1) >> 4

    wide = jnp.concatenate([notes] * (count // 128), 1) if count > 128 else notes
    place, unit, kind, group = where_from(wide.shape)
    match = (place == (plane ^ (group & (pop - 1)))) & ((unit & 1) == (core ^ (group >> (pop.bit_length() - 1))))
    total = jnp.sum(jnp.where(match & (kind == 0), wide, 0.0), 0, keepdims=True)
    rank = jnp.sum(jnp.where(match & (kind == 1) & (unit < 2), wide, 0.0), 0, keepdims=True)
    fitness = rank / (count - 1) - 0.5 + total / plays
    fitness = fitness * ((12.0 / count) ** 0.5)
    diag = lax.broadcasted_iota(i32, (count, count), 0) == lax.broadcasted_iota(i32, (count, count), 1)
    column = jnp.sum(jnp.where(diag, fitness, 0.0), 1, keepdims=True)
    weighted = post_ref[...].astype(f32) * column
    high = weighted.astype(bf16)
    both_ref[:count, :] = high
    both_ref[count:, :] = (weighted - high.astype(f32)).astype(bf16)

    inputs = pret_ref.shape[0]
    block = min(512, inputs)

    def out(i):
        at = block_rows(i, block)
        return pltpu.make_async_copy(grad_ref.at[at], grad_hbm.at[at], sems.at[i])

    def body(i, _):
        at = block_rows(i, block)
        pret = pret_ref[at, :]
        grad_ref[at, :] = dot(jnp.concatenate([pret, pret], 1), both_ref[...]).astype(bf16)
        out(i).start()
        return 0

    lax.fori_loop(0, inputs // block, body, 0, unroll=True)
    place, unit, kind, group = where_from(notes.shape)
    mine = (place == plane) & ((unit & 1) == group) & (kind == 0)
    ret_ref[...] = (jnp.sum(jnp.where(mine, notes, 0.0), 0, keepdims=True) / plays)[0, : ret_ref.shape[0]]
    lax.fori_loop(0, inputs // block, lambda i, _: (out(i).wait(), 0)[1], 0)


def grad_call(notes, pret, post, tp, pop, plays, members):
    inputs, count = pret.shape
    width = post.shape[1]
    return pl.pallas_call(
        functools.partial(grad_kernel, tp=tp, pop=pop, plays=plays),
        in_specs=[VM] * 3,
        out_specs=[HB, VM],
        out_shape=[sds((inputs, width), bf16), sds((members,), f32)],
        scratch_shapes=[
            pltpu.VMEM((2 * count, width), bf16),
            pltpu.VMEM((inputs, width), bf16),
            pltpu.SemaphoreType.DMA((inputs // min(512, inputs),)),
        ],
        name="grad",
        **params(16, 4 * inputs * count * width, 2 * inputs * (count + width)),
    )(notes, pret, post)


def swap(x, axis, mask):
    return lax.ppermute(x, axis, [(i, i ^ mask) for i in range(lax.axis_size(axis))])


def shards(
    in_spikes, w_in, w_rec, leak_rate, neuron_bias, readout, pert_table, pert_idx, member_ranks
):
    steps, epis, inputs = in_spikes.shape
    members = pert_idx.shape[0]
    tp, pop = lax.axis_size("tp"), lax.axis_size("pop")
    assert steps == 4 and epis < EP and members == 2 * EP

    w_sib = swap(w_rec, "tp", 1)
    side, load, post_loc = drive_call(
        in_spikes, w_in, neuron_bias, leak_rate, readout, pert_table, pert_idx, tp
    )
    got = lax.all_to_all(load, "tp", 0, 0)
    side_sib = swap(side, "tp", 1)
    base = base_call(got, w_rec, side)
    w_sib = tie_call(w_sib, base)
    w_own = swap(w_sib, "tp", 1)
    base = lax.all_to_all(base, "tp", 0, 0)
    proj1, pack = proj_call(got, post_loc)
    near = swap(pack, "pop", 1)
    s2o, s2s, memo, mems, s1c = step2_call(base, got, w_own, w_sib, proj1, side, side_sib, epis)
    far, order = [], []
    if tp == 8:
        xa, yb = swap(s2o, "tp", 2), swap(s2s, "tp", 4)
        xb, ya = swap(s2s, "tp", 2), swap(s2o, "tp", 4)
    else:
        for mask in range(2, tp, 2):
            far += [swap(s2o, "tp", mask), swap(s2s, "tp", mask)]
            order += [mask, mask + 1]
    acco, accs, proj, read, pair = own_call(
        s2o, s2s, w_own, w_sib, got, s1c, memo, mems, side, side_sib, pack, near, epis
    )
    if tp == 8:
        xa, yb = tie_call(xa, pair), tie_call(yb, pair)
        far, order = [xa, yb], [2, 5]
        end, ends = [swap(xa, "tp", 4), swap(yb, "tp", 2)], [6, 7]
    else:
        far, end, order, ends = far[:-2], far[-2:], order[:-2], order[-2:]
    acco, accs, proj, tail = part_call(far, order, w_own, w_sib, got, acco, accs, proj, tuple(ends))
    if tp == 8:
        acco, accs, proj = part_call([xb, ya], [3, 4], w_own, w_sib, got, acco, accs, proj)
    notes = last_call(
        end, ends, tail, got, acco, accs, proj, side, side_sib, read, member_ranks[None], epis, pop * tp
    )
    groups, mask = [pair], 2
    while mask < pop:
        groups += [swap(g, "pop", mask) for g in groups]
        mask *= 2
    groups += [swap(g, "tp", 1) for g in groups[:1]] + [swap(hand_call(g, notes), "tp", 1) for g in groups[1:]]
    notes = lax.all_to_all(notes, ("pop", "tp"), 0, 0, tiled=True)
    pret, post_all = prep_call(groups, pop)
    grad, returns = grad_call(notes, pret, post_all, tp, pop, epis * steps, members)
    return (returns, grad)


def solution(mesh):
    placed = (
        P(),
        P(None, "tp"),
        P(None, "tp"),
        P("tp"),
        P("tp"),
        P("tp"),
        P(None, "tp"),
        P("pop", None),
        P("pop"),
    )
    return jax.shard_map(
        shards, mesh=mesh, in_specs=placed, out_specs=(P("pop"), P(None, "tp")), check_vma=False
    )
```

```python
import functools

import jax
import jax.numpy as jnp
from jax import lax
from jax.experimental import pallas as pl
from jax.experimental.pallas import tpu as pltpu
from jax.sharding import PartitionSpec as P

sigma_scale = 0.01
f32 = jnp.float32
bf16 = jnp.bfloat16
i32 = jnp.int32
L_BASE = 58
L_STEP2 = 32
L_PART = 24
L_DRIVE = 58
L_LAST = 24
EP = 16


def spike(membrane):
    return (0.5 + 0.5 * jnp.tanh(2.0 * (membrane - 1.0))).astype(bf16)


def dot(a, b):
    return jnp.dot(a, b, preferred_element_type=f32)


def fold(x):
    parts = [x[:, i : i + 128] for i in range(0, x.shape[1], 128)]
    return functools.reduce(jnp.add, parts)


def params(mib, flops, nbytes):
    return dict(
        compiler_params=pltpu.CompilerParams(vmem_limit_bytes=mib * 2**20),
        cost_estimate=pl.CostEstimate(flops=flops, bytes_accessed=nbytes, transcendentals=0),
    )


VM = pl.BlockSpec(memory_space=pltpu.VMEM)
HB = pl.BlockSpec(memory_space=pltpu.HBM)
sds = jax.ShapeDtypeStruct


def block_rows(b, width):
    return pl.ds(pl.multiple_of(b * width, width), width)


def drive_kernel(
    spk_hbm, win_hbm, bias_hbm, leak_hbm, read_hbm, table_hbm, idx_hbm,
    side_ref, load_ref, post_ref,
    spk, win, bias, leak, read, table, idx, acc_ref, sems,
):
    epis, steps, inputs = spk.shape
    tp = load_ref.shape[0]
    parts = 8
    depth = inputs // parts
    copies = []
    for k in range(parts):
        at = pl.ds(k * depth, depth)
        copies.append((spk_hbm.at[:, :, at], spk.at[:, :, at]))
        copies.append((win_hbm.at[at], win.at[at]))
    copies += [(table_hbm, table), (idx_hbm, idx), (bias_hbm, bias), (leak_hbm, leak), (read_hbm, read)]
    copies = [pltpu.make_async_copy(a, b, sems.at[n]) for n, (a, b) in enumerate(copies)]
    for copy in copies:
        copy.start()
    for k in range(parts):
        copies[2 * k].wait()
        copies[2 * k + 1].wait()
        at = slice(k * depth, (k + 1) * depth)
        x = spk[:, :, at].reshape(epis * steps, depth).astype(f32).astype(bf16)
        part = dot(x, win[at, :])
        total = part if k == 0 else total + part
    for copy in copies[2 * parts :]:
        copy.wait()
    total = total + bias[...]
    lanes = range(acc_ref.shape[0])
    for c in lanes:
        acc_ref[c] = total[:, c * 128 : (c + 1) * 128]
    blank = jnp.zeros((EP - epis, total.shape[1]), f32)
    for t in range(steps):
        drive = jnp.concatenate([acc_ref[c, pl.ds(t, epis, stride=steps), :] for c in lanes], 1)
        drive = jnp.concatenate([drive, blank], 0)
        side_ref[t * EP : (t + 1) * EP, :] = drive
        if t == 0:
            s0 = spike(drive).astype(f32)
            here = lax.broadcasted_iota(i32, s0.shape, 0) < epis
            s0 = jnp.where(here, s0, 0.0).astype(bf16)
            for j in range(tp):
                load_ref[j, :EP, :] = s0
    row = lax.broadcasted_iota(i32, (8, total.shape[1]), 0)
    side_ref[steps * EP :, :] = jnp.where(row == 0, leak[...], read[...])
    at = lax.broadcasted_iota(i32, (table.shape[0], idx.shape[1]), 0)
    pick = (((0,), (0,)), ((), ()))
    pre, post = (
        lax.dot_general(
            jnp.where(at == idx[n : n + 1, :], 1.0, 0.0).astype(bf16), table[...], pick, preferred_element_type=f32
        ).astype(bf16)
        for n in range(2)
    )
    for j in range(tp):
        own = slice((j % 2) * EP, (j % 2 + 1) * EP)
        load_ref[j, EP : 2 * EP, :] = pre[own]
        load_ref[j, 2 * EP :, :] = post[own]
    for c in range(2):
        post_ref[c] = post[c * EP : (c + 1) * EP]


def drive_call(in_spikes, w_in, bias, leak, read, table, idx, tp):
    steps, epis, inputs = in_spikes.shape
    width = w_in.shape[1]
    members = idx.shape[0]
    ins = [in_spikes.transpose(1, 0, 2), w_in, bias[None], leak[None], read[None], table, idx.T]
    return pl.pallas_call(
        drive_kernel,
        in_specs=[HB] * 7,
        out_specs=[VM] * 3,
        out_shape=[
            sds((steps * EP + 8, width), f32),
            sds((tp, 3 * EP, width), bf16),
            sds((2, EP, width), bf16),
        ],
        scratch_shapes=[pltpu.VMEM(x.shape, x.dtype) for x in ins]
        + [pltpu.VMEM((width // 128, steps * epis, 128), f32), pltpu.SemaphoreType.DMA((21,))],
        name="drive",
        **params(L_DRIVE, 2 * steps * EP * inputs * width, inputs * width * 2 + steps * EP * inputs * 4),
    )(*ins)


def base_kernel(got_hbm, w_hbm, side_hbm, out_ref, got_ref, w_ref, side_ref, sems):
    tp, _, width = got_ref.shape
    lead = side_ref.shape[0] - 8
    copies = [(got_hbm.at[:, pl.ds(0, EP)], got_ref)]
    for j in range(tp):
        at = pl.ds(j * width, width)
        copies.append((w_hbm.at[at], w_ref.at[at]))
    copies.append((side_hbm, side_ref))
    copies = [pltpu.make_async_copy(a, b, sems.at[n]) for n, (a, b) in enumerate(copies)]
    for copy in copies:
        copy.start()
    copies[0].wait()
    base = jnp.zeros((EP, width), f32)
    for j in range(tp):
        copies[j + 1].wait()
        base += dot(got_ref[j], w_ref[j * width : (j + 1) * width, :])
    copies[-1].wait()
    mem0 = side_ref[0:EP, :]
    leak = side_ref[lead : lead + 1, :]
    base += leak * (mem0 - spike(mem0).astype(f32)) + side_ref[EP : 2 * EP, :]
    for i in range(tp):
        out_ref[i] = base


def base_call(got, w_rec, side):
    tp, _, width = got.shape
    return pl.pallas_call(
        base_kernel,
        in_specs=[HB, HB, HB],
        out_specs=VM,
        out_shape=sds((tp, EP, width), f32),
        scratch_shapes=[
            pltpu.VMEM((tp, EP, width), bf16),
            pltpu.VMEM(w_rec.shape, bf16),
            pltpu.VMEM(side.shape, f32),
            pltpu.SemaphoreType.DMA((tp + 2,)),
        ],
        name="base",
        **params(L_BASE, 2 * EP * tp * width * width, tp * width * width * 2),
    )(got, w_rec, side)


def proj_kernel(got_ref, post_ref, proj_ref, pack_ref):
    tp = got_ref.shape[0]
    proj = jnp.zeros((EP, EP), f32)
    for j in range(tp):
        pre = got_ref[j, EP : 2 * EP, :]
        proj += lax.dot_general(pre, got_ref[j, :EP, :], (((1,), (1,)), ((), ())), preferred_element_type=f32)
        pack_ref[j] = pre
    proj_ref[...] = sigma_scale * proj
    for c in range(2):
        pack_ref[tp + c] = post_ref[c]


def proj_call(got, post_loc):
    tp, _, width = got.shape
    return pl.pallas_call(
        proj_kernel,
        in_specs=[VM] * 2,
        out_specs=[VM] * 2,
        out_shape=[sds((EP, EP), f32), sds((tp + 2, EP, width), bf16)],
        name="proj",
        **params(8, 2 * EP * EP * tp * width, 4 * tp * EP * width),
    )(got, post_loc)


def step2_kernel(
    base_ref, rows_ref, wo_hbm, ws_hbm, proj1_ref, so_ref, ss_ref,
    s2o_ref, s2s_ref, memo_ref, mems_ref, s1c_ref,
    s1_ref, wo_ref, ws_ref, acco_ref, accs_ref, p2_ref, sems, *, epis,
):
    tp, _, width = base_ref.shape
    lead = so_ref.shape[0] - 8
    me = lax.axis_index("tp")

    def fetch(j):
        at = block_rows(j ^ me, width)
        return (
            pltpu.make_async_copy(wo_hbm.at[at], wo_ref.at[at], sems.at[0, j]),
            pltpu.make_async_copy(ws_hbm.at[at], ws_ref.at[at], sems.at[1, j]),
        )

    for j in range(tp):
        for copy in fetch(j):
            copy.start()

    def membrane1(b, e, post):
        return base_ref[b, e : e + 1, :] + proj1_ref[:, e : e + 1] * post

    p2_ref[...] = jnp.zeros_like(p2_ref)
    acco_ref[...] = jnp.zeros_like(acco_ref)
    accs_ref[...] = jnp.zeros_like(accs_ref)

    def rebuild(j):
        b = j ^ me
        pre = rows_ref[b, EP : 2 * EP, :].astype(f32)
        post = rows_ref[b, 2 * EP :, :].astype(f32)
        for e in range(epis):
            at = slice(e * EP, (e + 1) * EP)
            s1 = spike(membrane1(b, e, post))
            s1_ref[j, at, :] = s1
            p2_ref[at, :] += fold(s1.astype(f32) * pre)

    def multiply(j):
        for copy in fetch(j):
            copy.wait()
        at = block_rows(j ^ me, width)
        s1 = s1_ref[j]
        acco_ref[...] += dot(s1, wo_ref[at, :])
        accs_ref[...] += dot(s1, ws_ref[at, :])

    rebuild(0)

    def body(j, _):
        multiply(j)
        rebuild(j + 1)
        return 0

    lax.fori_loop(0, tp - 1, body, 0, unroll=True)
    multiply(tp - 1)
    proj2 = sigma_scale * jnp.sum(p2_ref[...], axis=1, keepdims=True)
    for h, side_ref, acc_ref, s2_ref, mem_ref in (
        (0, so_ref, acco_ref, s2o_ref, memo_ref),
        (1, ss_ref, accs_ref, s2s_ref, mems_ref),
    ):
        leak = side_ref[lead : lead + 1, :]
        post = rows_ref[h ^ me, 2 * EP :, :].astype(f32)
        for e in range(epis):
            at = slice(e * EP, (e + 1) * EP)
            s1 = s1_ref[h, at, :]
            s1c_ref[h, at, :] = s1
            mem = leak * (membrane1(h ^ me, e, post) - s1.astype(f32)) + side_ref[2 * EP + e : 2 * EP + e + 1, :]
            mem = mem + acc_ref[at, :] + proj2[at, :] * post
            mem_ref[at, :] = mem
            s2_ref[at, :] = spike(mem)


def step2_call(base, got, w_rec, w_sib, proj1, side, side_sib, epis):
    tp, _, width = base.shape
    n = epis * EP
    return pl.pallas_call(
        functools.partial(step2_kernel, epis=epis),
        in_specs=[VM, VM, HB, HB, VM, VM, VM],
        out_specs=[VM] * 5,
        out_shape=[
            sds((n, width), bf16), sds((n, width), bf16), sds((n, width), f32), sds((n, width), f32),
            sds((2, n, width), bf16),
        ],
        scratch_shapes=[
            pltpu.VMEM((tp, n, width), bf16),
            pltpu.VMEM(w_sib.shape, bf16),
            pltpu.VMEM(w_sib.shape, bf16),
            pltpu.VMEM((n, width), f32),
            pltpu.VMEM((n, width), f32),
            pltpu.VMEM((n, 128), f32),
            pltpu.SemaphoreType.DMA((2, tp)),
        ],
        name="step2",
        **params(L_STEP2, 4 * n * tp * width * width, 4 * tp * width * width),
    )(base, got, w_rec, w_sib, proj1, side, side_sib)


def fetch_blocks(order, me, wo_hbm, ws_hbm, w_ref, sems):
    copies = []
    for n, v in enumerate(order):
        at = block_rows(v ^ me, wo_hbm.shape[1])
        for h, hbm in ((0, wo_hbm), (1, ws_hbm)):
            copies.append(pltpu.make_async_copy(hbm.at[at], w_ref.at[h, n], sems.at[h, n]))
    for copy in copies:
        copy.start()
    return copies


def add_blocks(order, me, blocks, copies, w_ref, rows_ref, acco_ref, accs_ref, p_ref):
    for n, v in enumerate(order):
        for copy in copies[2 * n : 2 * n + 2]:
            copy.wait()
        block = blocks[n][...]
        acco_ref[...] += dot(block, w_ref[0, n])
        accs_ref[...] += dot(block, w_ref[1, n])
        pre = rows_ref[v ^ me, EP : 2 * EP, :].astype(f32)
        for r in range(0, block.shape[0], EP):
            p_ref[r : r + EP, :] += fold(block[r : r + EP, :].astype(f32) * pre)


def own_kernel(
    s2o_ref, s2s_ref, wo_hbm, ws_hbm, rows_ref, s1c_ref, memo_ref, mems_ref, so_ref, ss_ref, pack_ref, near_ref,
    acco_ref, accs_ref, p_ref, read_ref, pair_ref, w_ref, sems, *, epis,
):
    blocks = (s2o_ref, s2s_ref)
    width = wo_hbm.shape[1]
    lead = so_ref.shape[0] - 8
    me = lax.axis_index("tp")
    copies = fetch_blocks([0, 1], me, wo_hbm, ws_hbm, w_ref, sems)
    pair_ref[0] = pack_ref[...]
    pair_ref[1] = near_ref[...]
    p_ref[...] = jnp.zeros_like(p_ref)
    sums = jnp.zeros((EP, 128), f32)
    for h, side_ref, mem_ref, acc_ref in ((0, so_ref, memo_ref, acco_ref), (1, ss_ref, mems_ref, accs_ref)):
        leak, read = side_ref[lead : lead + 1, :], side_ref[lead + 1 : lead + 2, :]
        s0 = rows_ref[h ^ me, :EP, :].astype(f32)
        total = jnp.broadcast_to(jnp.sum(s0, 0, keepdims=True), (EP, width))
        for e in range(epis):
            at = slice(e * EP, (e + 1) * EP)
            s2 = blocks[h][at, :].astype(f32)
            total += s1c_ref[h, at, :].astype(f32) + s2
            acc_ref[at, :] = leak * (mem_ref[at, :] - s2) + side_ref[3 * EP + e : 3 * EP + e + 1, :]
        sums += fold(total * read)
    read_ref[...] = sums
    add_blocks([0, 1], me, blocks, copies, w_ref, rows_ref, acco_ref, accs_ref, p_ref)


def own_call(s2o, s2s, w_rec, w_sib, rows, s1c, memo, mems, side, side_sib, pack, near, epis):
    n, width = s2o.shape
    return pl.pallas_call(
        functools.partial(own_kernel, epis=epis),
        in_specs=[VM, VM, HB, HB] + [VM] * 8,
        out_specs=[VM] * 5,
        out_shape=[
            sds((n, width), f32), sds((n, width), f32), sds((n, 128), f32), sds((EP, 128), f32),
            sds((2,) + pack.shape, bf16),
        ],
        scratch_shapes=[pltpu.VMEM((2, 2, width, width), bf16), pltpu.SemaphoreType.DMA((2, 2))],
        name="own",
        **params(L_PART, 8 * n * width * width, 8 * width * width),
    )(s2o, s2s, w_rec, w_sib, rows, s1c, memo, mems, side, side_sib, pack, near)


def part_kernel(*refs, order, tail):
    blocks, refs = refs[: len(order)], refs[len(order) :]
    wo_hbm, ws_hbm, rows_ref, acco_in, accs_in, p_in, acco_ref, accs_ref, p_ref, *rest = refs
    w_ref, sems = rest[-2:]
    me = lax.axis_index("tp")
    copies = fetch_blocks(order, me, wo_hbm, ws_hbm, w_ref, sems)
    if tail:
        later = fetch_blocks(tail, me, wo_hbm, ws_hbm, rest[0], rest[1])
    acco_ref[...] = acco_in[...]
    accs_ref[...] = accs_in[...]
    p_ref[...] = p_in[...]
    add_blocks(order, me, blocks, copies, w_ref, rows_ref, acco_ref, accs_ref, p_ref)
    if tail:
        for copy in later:
            copy.wait()


def part_call(blocks, order, w_rec, w_sib, rows, acco, accs, proj, tail=()):
    n, width = blocks[0].shape
    count = len(order)
    more = [sds((2, len(tail), width, width), bf16)] if tail else []
    sems = [pltpu.SemaphoreType.DMA((2, len(tail)))] if tail else []
    return pl.pallas_call(
        functools.partial(part_kernel, order=order, tail=tail),
        in_specs=[VM] * count + [HB, HB] + [VM] * 4,
        out_specs=[VM] * (3 + len(more)),
        out_shape=[sds((n, width), f32), sds((n, width), f32), sds((n, 128), f32)] + more,
        scratch_shapes=sems + [pltpu.VMEM((2, count, width, width), bf16), pltpu.SemaphoreType.DMA((2, count))],
        name="part",
        **params(L_PART, 4 * n * count * width * width, 4 * count * width * width),
    )(*blocks, w_rec, w_sib, rows, acco, accs, proj)


def last_kernel(*refs, order, epis, copies):
    blocks, refs = refs[: len(order)], refs[len(order) :]
    w_ref, rows_ref, acco_in, accs_in, p_in, so_ref, ss_ref, read_ref, ranks_ref = refs[:9]
    note_ref, acco_ref, accs_ref, p_ref = refs[9:]
    lead = so_ref.shape[0] - 8
    me = lax.axis_index("tp")
    acco_ref[...] = acco_in[...]
    accs_ref[...] = accs_in[...]
    p_ref[...] = p_in[...]
    add_blocks(order, me, blocks, [], w_ref, rows_ref, acco_ref, accs_ref, p_ref)
    proj = sigma_scale * jnp.sum(p_ref[...], axis=1, keepdims=True)
    sums = read_ref[...]
    for h, side_ref, acc_ref in ((0, so_ref, acco_ref), (1, ss_ref, accs_ref)):
        read = side_ref[lead + 1 : lead + 2, :]
        post = rows_ref[h ^ me, 2 * EP :, :].astype(f32)
        total = jnp.zeros(post.shape, f32)
        for e in range(epis):
            at = slice(e * EP, (e + 1) * EP)
            total += spike(acc_ref[at, :] + proj[at, :] * post).astype(f32)
        sums += fold(total * read)
    sums = jnp.sum(sums, axis=1, keepdims=True)
    row = lax.broadcasted_iota(i32, (EP, 128), 0)
    lane = lax.broadcasted_iota(i32, (EP, 128), 1) & (EP - 1)
    flat = jnp.sum(jnp.where(row == lane, sums, 0.0), axis=0, keepdims=True)
    ranks = ranks_ref[...].astype(f32)
    wide = lax.broadcasted_iota(i32, (EP, 2 * EP), 1)
    chosen = wide == lax.broadcasted_iota(i32, (EP, 2 * EP), 0) + (me & 1) * EP
    mine = jnp.sum(jnp.where(chosen, ranks, 0.0), axis=1, keepdims=True)
    rank = jnp.sum(jnp.where(row == lane, mine, 0.0), axis=0, keepdims=True)
    odd = (lax.broadcasted_iota(i32, (2 * copies, 128), 0) & 1) == 1
    note_ref[...] = jnp.where(odd, rank, flat)


def last_call(blocks, order, tail, rows, acco, accs, proj, side, side_sib, read, ranks, epis, copies):
    n, width = blocks[0].shape
    count = len(order)
    return pl.pallas_call(
        functools.partial(last_kernel, order=order, epis=epis, copies=copies),
        in_specs=[VM] * (count + 9),
        out_specs=VM,
        out_shape=sds((2 * copies, 128), f32),
        scratch_shapes=[
            pltpu.VMEM((n, width), f32),
            pltpu.VMEM((n, width), f32),
            pltpu.VMEM((n, 128), f32),
        ],
        name="last",
        **params(L_LAST, int(0.75 * 8 * n * width * width), int(0.75 * 8 * width * width)),
    )(*blocks, tail, rows, acco, accs, proj, side, side_sib, read, ranks)


def tie_kernel(x_ref, after_ref, out_ref):
    pass


def tie_call(x, after):
    return pl.pallas_call(
        tie_kernel,
        in_specs=[HB, HB],
        out_specs=HB,
        out_shape=sds(x.shape, x.dtype),
        input_output_aliases={0: 0},
        name="tie",
        **params(8, 0, 1024),
    )(x, after)


def hand_kernel(x_ref, after_ref, out_ref):
    out_ref[...] = x_ref[...]


def hand_call(x, after):
    return pl.pallas_call(
        hand_kernel,
        in_specs=[VM, HB],
        out_specs=VM,
        out_shape=sds(x.shape, x.dtype),
        name="hand",
        **params(8, 0, 1024),
    )(x, after)


def prep_kernel(*refs, pop):
    groups, (pret_ref, post_ref) = refs[:pop], refs[pop:]
    tp = groups[0].shape[1] - 2
    width = groups[0].shape[3]
    for b in range(tp):
        cols = jnp.concatenate([g[i, b] for g in groups for i in range(2)], 0)
        pret_ref[b * width : (b + 1) * width, :] = cols.astype(f32).T.astype(bf16)
    for d in range(2):
        for s in range(pop):
            at = (d * pop + s) * EP
            post_ref[at : at + EP, :] = groups[s // 2][s % 2, tp + (d ^ (lax.axis_index("tp") & 1))]


def prep_call(groups, pop):
    _, blocks, _, width = groups[0].shape
    count = 2 * pop * EP
    return pl.pallas_call(
        functools.partial(prep_kernel, pop=pop),
        in_specs=[VM] * len(groups),
        out_specs=[VM] * 2,
        out_shape=[sds(((blocks - 2) * width, count), bf16), sds((count, width), bf16)],
        name="prep",
        **params(16, count * blocks * width, 4 * count * blocks * width),
    )(*groups)


def grad_kernel(note_ref, pret_ref, post_ref, grad_hbm, ret_ref, both_ref, grad_ref, sems, *, tp, pop, plays):
    count = post_ref.shape[0]
    plane, core = lax.axis_index("pop"), lax.axis_index("tp") & 1
    shift = tp.bit_length() - 1
    notes = note_ref[...]

    def where_from(shape):
        row = lax.broadcasted_iota(i32, shape, 0)
        return (row >> 1) >> shift, (row >> 1) & (tp - 1), row & 1, lax.broadcasted_iota(i32, shape, 1) >> 4

    wide = jnp.concatenate([notes] * (count // 128), 1) if count > 128 else notes
    place, unit, kind, group = where_from(wide.shape)
    spot = group & (pop - 1)
    away = (spot >> 1) | ((spot & 1) * (pop // 2))
    match = (place == (plane ^ away)) & ((unit & 1) == (core ^ (group >> (pop.bit_length() - 1))))
    total = jnp.sum(jnp.where(match & (kind == 0), wide, 0.0), 0, keepdims=True)
    rank = jnp.sum(jnp.where(match & (kind == 1) & (unit < 2), wide, 0.0), 0, keepdims=True)
    fitness = rank / (count - 1) - 0.5 + total / plays
    fitness = fitness * ((12.0 / count) ** 0.5)
    diag = lax.broadcasted_iota(i32, (count, count), 0) == lax.broadcasted_iota(i32, (count, count), 1)
    column = jnp.sum(jnp.where(diag, fitness, 0.0), 1, keepdims=True)
    weighted = post_ref[...].astype(f32) * column
    high = weighted.astype(bf16)
    both_ref[:count, :] = high
    both_ref[count:, :] = (weighted - high.astype(f32)).astype(bf16)

    inputs = pret_ref.shape[0]
    block = min(512, inputs)

    def out(i):
        at = block_rows(i, block)
        return pltpu.make_async_copy(grad_ref.at[at], grad_hbm.at[at], sems.at[i])

    def body(i, _):
        at = block_rows(i, block)
        pret = pret_ref[at, :]
        grad_ref[at, :] = dot(jnp.concatenate([pret, pret], 1), both_ref[...]).astype(bf16)
        out(i).start()
        return 0

    lax.fori_loop(0, inputs // block, body, 0, unroll=True)
    place, unit, kind, group = where_from(notes.shape)
    mine = (place == plane) & ((unit & 1) == group) & (kind == 0)
    ret_ref[...] = (jnp.sum(jnp.where(mine, notes, 0.0), 0, keepdims=True) / plays)[0, : ret_ref.shape[0]]
    lax.fori_loop(0, inputs // block, lambda i, _: (out(i).wait(), 0)[1], 0)


def grad_call(notes, pret, post, tp, pop, plays, members):
    inputs, count = pret.shape
    width = post.shape[1]
    return pl.pallas_call(
        functools.partial(grad_kernel, tp=tp, pop=pop, plays=plays),
        in_specs=[VM] * 3,
        out_specs=[HB, VM],
        out_shape=[sds((inputs, width), bf16), sds((members,), f32)],
        scratch_shapes=[
            pltpu.VMEM((2 * count, width), bf16),
            pltpu.VMEM((inputs, width), bf16),
            pltpu.SemaphoreType.DMA((inputs // min(512, inputs),)),
        ],
        name="grad",
        **params(16, 4 * inputs * count * width, 2 * inputs * (count + width)),
    )(notes, pret, post)


def swap(x, axis, mask):
    return lax.ppermute(x, axis, [(i, i ^ mask) for i in range(lax.axis_size(axis))])


def shards(
    in_spikes, w_in, w_rec, leak_rate, neuron_bias, readout, pert_table, pert_idx, member_ranks
):
    steps, epis, inputs = in_spikes.shape
    members = pert_idx.shape[0]
    tp, pop = lax.axis_size("tp"), lax.axis_size("pop")
    assert steps == 4 and epis < EP and members == 2 * EP

    w_sib = swap(w_rec, "tp", 1)
    side, load, post_loc = drive_call(
        in_spikes, w_in, neuron_bias, leak_rate, readout, pert_table, pert_idx, tp
    )
    got = lax.all_to_all(load, "tp", 0, 0)
    side_sib = swap(side, "tp", 1)
    base = base_call(got, w_rec, side)
    w_sib = tie_call(w_sib, base)
    w_own = swap(w_sib, "tp", 1)
    base = lax.all_to_all(base, "tp", 0, 0)
    proj1, pack = proj_call(got, post_loc)
    near = swap(pack, "pop", pop // 2)
    s2o, s2s, memo, mems, s1c = step2_call(base, got, w_own, w_sib, proj1, side, side_sib, epis)
    far, order = [], []
    if tp == 8:
        xa, yb = swap(s2o, "tp", 2), swap(s2s, "tp", 4)
        xb, ya = swap(s2s, "tp", 2), swap(s2o, "tp", 4)
    else:
        for mask in range(2, tp, 2):
            far += [swap(s2o, "tp", mask), swap(s2s, "tp", mask)]
            order += [mask, mask + 1]
    acco, accs, proj, read, pair = own_call(
        s2o, s2s, w_own, w_sib, got, s1c, memo, mems, side, side_sib, pack, near, epis
    )
    if tp == 8:
        xa, yb = tie_call(xa, pair), tie_call(yb, pair)
        far, order = [xa, yb], [2, 5]
        end, ends = [swap(xa, "tp", 4), swap(yb, "tp", 2)], [6, 7]
    else:
        far, end, order, ends = far[:-2], far[-2:], order[:-2], order[-2:]
    acco, accs, proj, tail = part_call(far, order, w_own, w_sib, got, acco, accs, proj, tuple(ends))
    if tp == 8:
        acco, accs, proj = part_call([xb, ya], [3, 4], w_own, w_sib, got, acco, accs, proj)
    notes = last_call(
        end, ends, tail, got, acco, accs, proj, side, side_sib, read, member_ranks[None], epis, pop * tp
    )
    groups, mask = [pair], 1
    while mask < pop // 2:
        groups += [swap(g, "pop", mask) for g in groups]
        mask *= 2
    groups += [swap(g, "tp", 1) for g in groups[:1]] + [swap(hand_call(g, notes), "tp", 1) for g in groups[1:]]
    notes = lax.all_to_all(notes, ("pop", "tp"), 0, 0, tiled=True)
    pret, post_all = prep_call(groups, pop)
    grad, returns = grad_call(notes, pret, post_all, tp, pop, epis * steps, members)
    return (returns, grad)


def solution(mesh):
    placed = (
        P(),
        P(None, "tp"),
        P(None, "tp"),
        P("tp"),
        P("tp"),
        P("tp"),
        P(None, "tp"),
        P("pop", None),
        P("pop"),
    )
    return jax.shard_map(
        shards, mesh=mesh, in_specs=placed, out_specs=(P("pop"), P(None, "tp")), check_vma=False
    )
```
